32 devices in a mesh: ctx: 8 (over z, y), head: 4 (over x, core).
Axes of the slice: x: 2, y: 2, z: 4, core: 2. Of those that a mesh axis runs over, the one named last changes fastest.
Arguments:
- queries: bfloat16 [3, 8, 8192], P(None, None, 'head'), may hold values from -8 to 8
- k_cache: bfloat16 [8, 2048, 1024], P(None, 'ctx', 'head'), may hold values from -6 to 6
- v_cache: bfloat16 [8, 2048, 1024], P(None, 'ctx', 'head'), may hold values from -6 to 6
- new_keys: bfloat16 [3, 8, 1024], P(None, None, 'head'), may hold values from -6 to 6
- new_values: bfloat16 [3, 8, 1024], P(None, None, 'head'), may hold values from -6 to 6
- fill: int32 [8, 8], P(None, 'ctx'), may hold values from 2 to 253, as said below
- owner: int32 [3, 8], replicated, may hold values from 0 to 7
- out_weight: bfloat16 [8192, 8192], P('head', 'ctx'), may hold values from -0.09375 to 0.09375
Outputs:
- keys_out: bfloat16 [8, 2048, 1024], P(None, 'ctx', 'head')
- values_out: bfloat16 [8, 2048, 1024], P(None, 'ctx', 'head')
- mixed: bfloat16 [3, 8, 8192], P(None, None, ('ctx', 'head'))
The draws below stay inside these ranges and needn't reach their ends.
Inputs may be any that keep to these rules, and one draw needn't show every extreme that they name: Rows 0 to fill - 1 of each shard hold the sequence's earlier positions; some entry equals 253.
All inputs are finite; a program needn't handle non-finite values.
Results may differ from the reference program's by a relative error of at most 0.0051.
Values may be sent and summed in bfloat16 or wider, within the bound.
A program may use at most 128 MiB of HBM per device.

```python
import jax
import jax.numpy as jnp
from jax import lax

D = 8192
HQ = 64
KVH = 8
HD = 128
BATCH = 8
ROWS = 256
STEPS = 3
CONTEXT = 2048
N_CTX = 8


def draw_queries(key, part):
    key = jax.random.fold_in(key, 11)
    base = jnp.clip(2.0 * jax.random.normal(key, (STEPS, BATCH, HQ * HD), jnp.float32), -8.0, 8.0)
    return base.astype(jnp.bfloat16)


def draw_k_cache(key, part):
    key = jax.random.fold_in(key, 12)
    base = jnp.clip(jax.random.normal(key, (BATCH, CONTEXT, KVH * HD), jnp.float32), -6.0, 6.0)
    return base.astype(jnp.bfloat16)


def draw_fill(key, part):
    key = jax.random.fold_in(key, 13)
    shards = CONTEXT // ROWS
    most = ROWS - STEPS
    values = jax.random.randint(key, (BATCH, shards), 2, most + 1)
    which_row = jax.random.randint(jax.random.fold_in(key, 1), (), 0, BATCH)
    which_shard = jax.random.randint(jax.random.fold_in(key, 2), (), 0, shards)
    row_ids = jax.lax.broadcasted_iota(jnp.int32, (BATCH, shards), 0)
    shard_ids = jax.lax.broadcasted_iota(jnp.int32, (BATCH, shards), 1)
    chosen = (row_ids == which_row) & (shard_ids == which_shard)
    return jnp.where(chosen, most, values).astype(jnp.int32)


def place_ends(values, stream_key, low, high):
    dims = values.shape
    spot = [jax.random.randint(jax.random.fold_in(stream_key, axis), (), 0, dims[axis]) for axis in range(len(dims))]
    values = values.at[tuple(spot)].set(low)
    longest = dims.index(max(dims))
    spot[longest] = (spot[longest] + 1) % dims[longest]
    return values.at[tuple(spot)].set(high)


def strengthened(entries, key, source, target, blocks, factor):
    owner, partner = [(jnp.arange(entries.shape[position]) // (entries.shape[position] // blocks)).reshape([-1 if axis == position else 1 for axis in range(entries.ndim)]) for position in (source, target)]
    chosen = jax.random.permutation(key, blocks)[partner]
    strong = (owner == chosen) | (owner == (partner + blocks // 2) % blocks)
    return jnp.where(strong, factor * entries, entries)


def shard_levels(rng, extent, cuts, smallest, high):
    loudness = 1.0
    for position, blocks in cuts:
        steps = jax.random.uniform(jax.random.fold_in(jax.random.fold_in(rng, 6), position), (blocks,), jnp.float32, smallest / len(cuts), high / len(cuts))
        loudness = loudness * jnp.repeat(jnp.exp(steps), extent[position] // blocks).reshape((-1,) + (1,) * (len(extent) - 1 - position))
    return loudness


def gaussian(own_key, extent, scale, limit, pieces=(), kind=jnp.bfloat16):
    level = shard_levels(own_key, extent, pieces, -0.22, 0.18) if pieces else 1.0
    values = jax.random.normal(own_key, extent, jnp.float32) * scale * level
    return jnp.minimum(jnp.maximum(values, -limit), limit).astype(kind)


def noise_with(stream_key, extent, width, bound, pieces, heavy, kind=jnp.bfloat16):
    values = width * jax.random.normal(stream_key, extent, jnp.float32)
    if pieces:
        values = values * shard_levels(stream_key, extent, pieces, -0.22, 0.18)
    return jnp.clip(strengthened(values, jax.random.fold_in(stream_key, 3), *heavy), -bound, bound).astype(kind)


def setup_inputs(seed: int = 0) -> dict:
    keys = jax.random.split(jax.random.key(seed), 9)
    queries = draw_queries(jax.random.fold_in(keys[8], 71), 0)
    k_cache = draw_k_cache(jax.random.fold_in(keys[8], 71), 0)
    v_cache = gaussian(keys[2], (BATCH, CONTEXT, KVH * HD), 1.0, 6.0, ((1, 8), (2, 4)))
    new_keys = gaussian(keys[3], (STEPS, BATCH, KVH * HD), 1.0, 6.0, ((2, 4),))
    new_values = gaussian(keys[4], (STEPS, BATCH, KVH * HD), 1.0, 6.0, ((2, 4),))
    fill = draw_fill(jax.random.fold_in(keys[8], 71), 0)
    owner = place_ends(jax.random.randint(keys[6], (STEPS, BATCH), 0, N_CTX), jax.random.fold_in(keys[6], 1), 0, N_CTX - 1).astype(jnp.int32)
    out_weight = noise_with(keys[7], (D, D), D ** -0.5, 0.09375, ((0, 4), (1, 8)), (0, 1, 8, 2.0))
    return {"queries": queries, "k_cache": k_cache, "v_cache": v_cache, "new_keys": new_keys, "new_values": new_values, "fill": fill, "owner": owner, "out_weight": out_weight}


def attend(packed):
    query_rows, key_rows, value_rows, live_len = packed
    groups = HQ // KVH
    shards = key_rows.shape[0] // ROWS
    query_heads = query_rows.reshape(STEPS, KVH, groups, HD).astype(jnp.float32)
    key_heads = key_rows.reshape(shards, ROWS, KVH, HD).astype(jnp.float32)
    value_heads = value_rows.reshape(shards, ROWS, KVH, HD).astype(jnp.float32)
    scores = jnp.einsum('sgqd,crgd->sgqcr', query_heads, key_heads) * (1.0 / HD ** 0.5)
    slots = jnp.arange(ROWS, dtype=jnp.int32)
    live = (slots[None, None, :] < live_len[:, :, None])[:, None, None, :, :]
    masked = jnp.where(live, scores, -1e30)
    peak = jnp.max(masked, axis=-1)
    weights = jnp.where(live, jnp.exp(masked - peak[..., None]), 0.0)
    total = jnp.sum(weights, axis=-1)
    rounded = weights.astype(jnp.bfloat16)
    rounded = lax.optimization_barrier(rounded).astype(jnp.float32)
    part = jnp.einsum('sgqcr,crgd->sgqcd', rounded, value_heads)
    largest = jnp.max(peak, axis=-1)
    factor = jnp.exp(peak - largest[..., None])
    numer = jnp.sum(part * factor[..., None], axis=-2)
    denom = jnp.sum(total * factor, axis=-1)
    return (numer / denom[..., None]).astype(jnp.bfloat16).reshape(STEPS, HQ * HD)


def reference(queries, k_cache, v_cache, new_keys, new_values, fill, owner, out_weight):
    shards = fill.shape[1]
    batch_ids = jnp.arange(BATCH, dtype=jnp.int32)
    onehot = (owner[:, :, None] == jnp.arange(shards, dtype=jnp.int32)[None, None, :]).astype(jnp.int32)
    counted = jnp.cumsum(onehot, axis=0).astype(jnp.int32)
    keys_out, values_out = k_cache, v_cache
    for step in range(STEPS):
        target = owner[step]
        base_fill = jnp.take_along_axis(fill, target[:, None], axis=1)[:, 0]
        seen = jnp.take_along_axis(counted[step], target[:, None], axis=1)[:, 0]
        row_index = (target * ROWS + base_fill + seen - 1).astype(jnp.int32)
        keys_out = keys_out.at[batch_ids, row_index].set(new_keys[step])
        values_out = values_out.at[batch_ids, row_index].set(new_values[step])
    lengths = (fill[None, :, :] + counted).astype(jnp.int32)
    attention = lax.map(attend, (jnp.transpose(queries, (1, 0, 2)), keys_out, values_out, jnp.transpose(lengths, (1, 0, 2))))
    attention = jnp.transpose(attention, (1, 0, 2)).reshape(STEPS * BATCH, HQ * HD)
    mixed = jnp.dot(attention, out_weight, preferred_element_type=jnp.float32).astype(jnp.bfloat16)
    return keys_out, values_out, mixed.reshape(STEPS, BATCH, D)
```

```python
import functools

import jax
import jax.numpy as jnp
from jax import lax
from jax.experimental import pallas as pl
from jax.experimental.pallas import tpu as pltpu
from jax.sharding import PartitionSpec as P

HD = 128


def on_device(queries, k_cache, v_cache, new_keys, new_values, fill, owner, out_weight):
    steps, batch = owner.shape
    rows = k_cache.shape[1]
    device_pos = lax.axis_index("ctx")
    mine = (owner == device_pos).astype(jnp.int32)
    seen = jnp.cumsum(mine, axis=0)
    local_fill = fill[:, 0]
    slot = local_fill[None, :] + seen - 1
    row_ids = lax.broadcasted_iota(jnp.int32, (batch, rows), 1)
    keys_out, values_out = (k_cache, v_cache)
    for step in range(steps):
        target = ((row_ids == slot[step][:, None]) & (mine[step][:, None] == 1))[:, :, None]
        keys_out = jnp.where(target, new_keys[step][:, None, :], keys_out)
        values_out = jnp.where(target, new_values[step][:, None, :], values_out)
    lengths = local_fill[None, :] + seen
    kv_local = keys_out.shape[2] // HD
    groups = queries.shape[2] // (kv_local * HD)
    query_heads = queries.reshape(steps, batch, kv_local, groups, HD)
    key_heads = keys_out.reshape(batch, rows, kv_local, HD)
    value_heads = values_out.reshape(batch, rows, kv_local, HD)
    scores = jnp.einsum(
        "sbgqd,brgd->sbgqr", query_heads, key_heads, preferred_element_type=jnp.float32
    ) * (1.0 / HD**0.5)
    slot_ids = lax.broadcasted_iota(jnp.int32, (1, 1, 1, 1, rows), 4)
    live = slot_ids < lengths[:, :, None, None, None]
    masked = jnp.where(live, scores, -1e30)
    peak = jnp.max(masked, axis=-1)
    weights = jnp.where(live, jnp.exp(masked - peak[..., None]), 0.0)
    total = jnp.sum(weights, axis=-1)
    rounded = weights.astype(jnp.bfloat16)
    numer = jnp.einsum(
        "sbgqr,brgd->sbgqd", rounded, value_heads, preferred_element_type=jnp.float32
    )
    largest = lax.pmax(peak, "ctx")
    factor = jnp.exp(peak - largest)
    numer_all, total_all = lax.psum((numer * factor[..., None], total * factor), "ctx")
    attention = (numer_all / total_all[..., None]).astype(jnp.bfloat16)
    attention_rows = attention.reshape(steps * batch, kv_local * groups * HD)
    partial_out = jnp.dot(attention_rows, out_weight, preferred_element_type=jnp.float32)
    mixed = lax.psum_scatter(partial_out, "head", scatter_dimension=1, tiled=True).astype(
        jnp.bfloat16
    )
    return (keys_out, values_out, mixed.reshape(steps, batch, -1))


MESH = pl.DeviceIdType.MESH
STAT_ROWS = 16


def new_rows(old, slots, rows_f32, step_rows):
    ids = lax.broadcasted_iota(jnp.int32, old.shape, 0)
    out = old.astype(jnp.float32)
    for slot, row in zip(slots, step_rows):
        out = jnp.where(ids == slot, rows_f32[row : row + 1, :], out)
    return out.astype(old.dtype)


def fused_kernel(
    n_ctx, n_head, steps, batch, groups, kv_local,
    fill, owner, q_hbm, k_hbm, v_hbm, nk_hbm, nv_hbm, w_hbm,
    k_out, v_out, mixed,
    q_v, nk_v, nv_v, k_v, v_v, w_v, q_rows, part, stat, nk_f, nv_f,
    send1, recv1, send2, recv2, send3, recv3,
    small_sem, k_sem, v_sem, w_sem, ko_sem, vo_sem,
    ssem1, rsem1, ssem2, rsem2, ssem3, rsem3,
):
    me = lax.axis_index("ctx")
    hme = lax.axis_index("head")
    tokens = steps * batch
    rows = k_v.shape[1]
    heads = groups * kv_local
    per = heads // n_ctx
    block = per * tokens
    depth = per * HD
    width = mixed.shape[2]

    barrier = pltpu.get_barrier_semaphore()
    for d in range(1, n_ctx):
        pl.semaphore_signal(barrier, inc=1, device_id={"ctx": lax.rem(me + d, n_ctx)}, device_id_type=MESH)
    for d in range(1, n_head):
        pl.semaphore_signal(barrier, inc=1, device_id={"head": lax.rem(hme + d, n_head)}, device_id_type=MESH)

    smalls = [
        pltpu.make_async_copy(q_hbm, q_v, small_sem.at[0]),
        pltpu.make_async_copy(nk_hbm, nk_v, small_sem.at[1]),
        pltpu.make_async_copy(nv_hbm, nv_v, small_sem.at[2]),
    ]
    k_in = [pltpu.make_async_copy(k_hbm.at[b], k_v.at[b], k_sem.at[b]) for b in range(batch)]
    v_in = [pltpu.make_async_copy(v_hbm.at[b], v_v.at[b], v_sem.at[b]) for b in range(batch)]
    w_in = [
        pltpu.make_async_copy(w_hbm.at[pl.ds(c * depth, depth), :], w_v.at[c], w_sem.at[c])
        for c in range(n_ctx)
    ]
    for copy in smalls:
        copy.start()
    for b in range(batch):
        k_in[b].start()
        v_in[b].start()
    for copy in w_in:
        copy.start()

    smalls[0].wait()
    for s in range(steps):
        q_f = q_v[s].astype(jnp.float32)
        for h in range(heads):
            q_rows[h * tokens + s * batch : h * tokens + (s + 1) * batch, :] = q_f[:, h * HD : (h + 1) * HD]
    smalls[1].wait()
    smalls[2].wait()
    for s in range(steps):
        nk_f[s * batch : (s + 1) * batch, :] = nk_v[s].astype(jnp.float32)
        nv_f[s * batch : (s + 1) * batch, :] = nv_v[s].astype(jnp.float32)

    live_rows = groups * steps
    step_ids = lax.rem(lax.broadcasted_iota(jnp.int32, (live_rows, rows), 0), steps)
    slot_ids = lax.broadcasted_iota(jnp.int32, (live_rows, rows), 1)
    lane = lax.broadcasted_iota(jnp.int32, (live_rows, HD), 1)
    pick = (
        lax.broadcasted_iota(jnp.int32, (STAT_ROWS, HD), 0)
        == lax.broadcasted_iota(jnp.int32, (STAT_ROWS, HD), 1)
    ).astype(jnp.bfloat16)

    slots, lengths = [], []
    for b in range(batch):
        seen = fill[b, 0]
        slots_b, lengths_b = [], []
        for s in range(steps):
            mine = owner[s, b] == me
            slots_b.append(jnp.where(mine, seen, -1))
            seen = seen + jnp.where(mine, 1, 0)
            lengths_b.append(seen)
        slots.append(slots_b)
        lengths.append(lengths_b)

    first = [
        [
            pltpu.make_async_remote_copy(
                src_ref=send1.at[c],
                dst_ref=recv1.at[lax.rem(c - me + n_ctx, n_ctx)],
                send_sem=ssem1.at[c],
                recv_sem=rsem1.at[lax.rem(c - me + n_ctx, n_ctx)],
                device_id={"ctx": c},
                device_id_type=MESH,
            )
        ]
        for c in range(n_ctx)
    ]
    sent = 0
    for g in range(kv_local):
        cols = slice(g * HD, (g + 1) * HD)
        nk_g, nv_g = nk_f[:, cols], nv_f[:, cols]
        for b in range(batch):
            at = pl.ds(g * groups * tokens + b, live_rows, stride=batch)
            step_rows = [s * batch + b for s in range(steps)]
            if g == 0:
                k_in[b].wait()
                v_in[b].wait()
            keys = new_rows(k_v[b, :, cols], slots[b], nk_g, step_rows)
            values = new_rows(v_v[b, :, cols], slots[b], nv_g, step_rows)
            k_v[b, :, cols] = keys
            v_v[b, :, cols] = values
            if g == kv_local - 1:
                pltpu.make_async_copy(k_v.at[b], k_out.at[b], ko_sem.at[b]).start()
                pltpu.make_async_copy(v_v.at[b], v_out.at[b], vo_sem.at[b]).start()
            query = q_rows[at, :].astype(jnp.bfloat16)
            scores = lax.dot_general(
                query, keys, (((1,), (1,)), ((), ())), preferred_element_type=jnp.float32
            ) * (1.0 / HD**0.5)
            length = jnp.full((live_rows, rows), lengths[b][steps - 1], jnp.int32)
            for s in range(steps - 1):
                length = jnp.where(step_ids == s, lengths[b][s], length)
            live = slot_ids < length
            masked = jnp.where(live, scores, -1e30)
            peak = jnp.max(masked, axis=1, keepdims=True)
            weights = jnp.where(live, jnp.exp(masked - peak), 0.0)
            total = jnp.sum(weights, axis=1, keepdims=True)
            part[at, :] = jnp.dot(
                weights.astype(jnp.bfloat16), values, preferred_element_type=jnp.float32
            )
            both = jnp.where(lax.rem(lane, 2) == 0, peak, total)
            high = both.astype(jnp.bfloat16).astype(jnp.float32)
            middle = (both - high).astype(jnp.bfloat16).astype(jnp.float32)
            low = both - high - middle
            stat[at, :] = jnp.where(lane < 2, high, jnp.where(lane < 4, middle, low))
        if g == 0:
            pl.semaphore_wait(barrier, n_ctx + n_head - 2)
        ready = n_ctx * (g + 1) // kv_local
        for c in range(sent, ready):
            here = slice(c * block, (c + 1) * block)
            send1[c, 0:block, :] = part[here, :].astype(jnp.bfloat16)
            turned = lax.dot_general(
                pick, stat[here, :].astype(jnp.bfloat16), (((1,), (1,)), ((), ())),
                preferred_element_type=jnp.float32,
            )
            send1[c, block : block + STAT_ROWS, 0:block] = turned.astype(jnp.bfloat16)

            @pl.when(me != c)
            def _():
                first[c][0].start()

        sent = ready

    recv1[0] = send1[me]
    for d in range(1, n_ctx):
        pltpu.make_async_remote_copy(
            src_ref=send1.at[0], dst_ref=recv1.at[d], send_sem=ssem1.at[0], recv_sem=rsem1.at[d],
            device_id={"ctx": lax.rem(me + d, n_ctx)}, device_id_type=MESH,
        ).wait_recv()
    peaks, totals = [], []
    for d in range(n_ctx):
        got = recv1[d, block : block + STAT_ROWS, 0:block].astype(jnp.float32)
        peaks.append(got[0:1] + got[2:3] + got[4:5])
        totals.append(got[1:2] + got[3:4] + got[5:6])
    peaks = jnp.concatenate(peaks, axis=0)
    totals = jnp.concatenate(totals, axis=0)
    factor = jnp.exp(peaks - jnp.max(peaks, axis=0, keepdims=True))
    shares = factor / jnp.sum(factor * totals, axis=0, keepdims=True)
    shares = jnp.transpose(shares)
    attention = jnp.zeros((block, HD), jnp.float32)
    for d in range(n_ctx):
        attention += recv1[d, 0:block, :].astype(jnp.float32) * shares[:, d : d + 1]
    send2[...] = attention.astype(jnp.bfloat16)

    second = []
    for d in range(1, n_ctx):
        copy = pltpu.make_async_remote_copy(
            src_ref=send2, dst_ref=recv2.at[d], send_sem=ssem2.at[d], recv_sem=rsem2.at[d],
            device_id={"ctx": lax.rem(me + d, n_ctx)}, device_id_type=MESH,
        )
        copy.start()
        second.append(copy)
    for copy in w_in:
        copy.wait()
    share = None
    for d in range(n_ctx):
        if d > 0:
            second[d - 1].wait_recv()
            got = recv2[d].astype(jnp.float32)
        else:
            got = send2[...].astype(jnp.float32)
        features = jnp.concatenate(
            [got[i * tokens : (i + 1) * tokens] for i in range(per)], axis=1
        ).astype(jnp.bfloat16)
        product = jnp.dot(
            features, w_v[lax.rem(me - d + n_ctx, n_ctx)], preferred_element_type=jnp.float32
        )
        share = product if share is None else share + product
    for h in range(n_head):
        send3[h] = share[:, h * width : (h + 1) * width]
    third = []
    for d in range(1, n_head):
        target = lax.rem(hme + d, n_head)
        copy = pltpu.make_async_remote_copy(
            src_ref=send3.at[target], dst_ref=recv3.at[d], send_sem=ssem3.at[d], recv_sem=rsem3.at[d],
            device_id={"head": target}, device_id_type=MESH,
        )
        copy.start()
        third.append(copy)
    result = send3[hme]
    for copy in third:
        copy.wait_recv()
    for d in range(1, n_head):
        result += recv3[d]
    result = result.astype(mixed.dtype)
    for s in range(steps):
        mixed[s] = result[s * batch : (s + 1) * batch]

    for c in range(n_ctx):

        @pl.when(me != c)
        def _():
            first[c][0].wait_send()

    for copy in second:
        copy.wait_send()
    for copy in third:
        copy.wait_send()
    for b in range(batch):
        pltpu.make_async_copy(k_v.at[b], k_out.at[b], ko_sem.at[b]).wait()
        pltpu.make_async_copy(v_v.at[b], v_out.at[b], vo_sem.at[b]).wait()


def on_device_fused(
    n_ctx, n_head, queries, k_cache, v_cache, new_keys, new_values, fill, owner, out_weight
):
    steps, batch, features = queries.shape
    rows, kv_width = k_cache.shape[1:]
    kv_local = kv_width // HD
    heads = features // HD
    tokens = steps * batch
    columns = out_weight.shape[1]
    per = heads // n_ctx
    block = per * tokens
    if heads % n_ctx or block % 16 or block > HD or n_ctx % kv_local or batch != 8 or columns % (n_head * HD):
        return on_device(
            queries, k_cache, v_cache, new_keys, new_values, fill, owner, out_weight
        )
    kernel = functools.partial(
        fused_kernel, n_ctx, n_head, steps, batch, heads // kv_local, kv_local
    )
    whole = pl.BlockSpec(memory_space=pl.ANY)
    scalars = pl.BlockSpec(memory_space=pltpu.SMEM)
    dma = pltpu.SemaphoreType.DMA
    return pl.pallas_call(
        kernel,
        out_shape=(
            jax.ShapeDtypeStruct(k_cache.shape, k_cache.dtype),
            jax.ShapeDtypeStruct(v_cache.shape, v_cache.dtype),
            jax.ShapeDtypeStruct((steps, batch, columns // n_head), jnp.bfloat16),
        ),
        in_specs=[scalars, scalars] + [whole] * 6,
        out_specs=(whole, whole, pl.BlockSpec(memory_space=pltpu.VMEM)),
        scratch_shapes=[
            pltpu.VMEM(queries.shape, jnp.bfloat16),
            pltpu.VMEM(new_keys.shape, jnp.bfloat16),
            pltpu.VMEM(new_values.shape, jnp.bfloat16),
            pltpu.VMEM(k_cache.shape, jnp.bfloat16),
            pltpu.VMEM(v_cache.shape, jnp.bfloat16),
            pltpu.VMEM((n_ctx, per * HD, columns), jnp.bfloat16),
            pltpu.VMEM((heads * tokens, HD), jnp.float32),
            pltpu.VMEM((heads * tokens, HD), jnp.float32),
            pltpu.VMEM((heads * tokens, HD), jnp.float32),
            pltpu.VMEM((tokens, kv_width), jnp.float32),
            pltpu.VMEM((tokens, kv_width), jnp.float32),
            pltpu.VMEM((n_ctx, block + STAT_ROWS, HD), jnp.bfloat16),
            pltpu.VMEM((n_ctx, block + STAT_ROWS, HD), jnp.bfloat16),
            pltpu.VMEM((block, HD), jnp.bfloat16),
            pltpu.VMEM((n_ctx, block, HD), jnp.bfloat16),
            pltpu.VMEM((n_head, tokens, columns // n_head), jnp.float32),
            pltpu.VMEM((n_head, tokens, columns // n_head), jnp.float32),
            dma((3,)),
            dma((batch,)),
            dma((batch,)),
            dma((n_ctx,)),
            dma((batch,)),
            dma((batch,)),
            dma((n_ctx,)),
            dma((n_ctx,)),
            dma((n_ctx,)),
            dma((n_ctx,)),
            dma((n_head,)),
            dma((n_head,)),
        ],
        compiler_params=pltpu.CompilerParams(
            collective_id=0, has_side_effects=True, vmem_limit_bytes=48 * 1024 * 1024
        ),
        cost_estimate=pl.CostEstimate(
            flops=2 * tokens * features * (columns + 2 * rows),
            bytes_accessed=2 * (2 * k_cache.size + 2 * v_cache.size + out_weight.size),
            transcendentals=tokens * heads * rows,
        ),
    )(fill, owner, queries, k_cache, v_cache, new_keys, new_values, out_weight)


def solution(mesh):
    in_specs = (
        P(None, None, "head"),
        P(None, "ctx", "head"),
        P(None, "ctx", "head"),
        P(None, None, "head"),
        P(None, None, "head"),
        P(None, "ctx"),
        P(),
        P("head", "ctx"),
    )
    out_specs = (P(None, "ctx", "head"), P(None, "ctx", "head"), P(None, None, ("ctx", "head")))
    return jax.shard_map(
        functools.partial(on_device_fused, mesh.shape["ctx"], mesh.shape["head"]), mesh=mesh, in_specs=in_specs, out_specs=out_specs, check_vma=False
    )
```

```python
import functools

import jax
import jax.numpy as jnp
from jax import lax
from jax.experimental import pallas as pl
from jax.experimental.pallas import tpu as pltpu
from jax.sharding import PartitionSpec as P

HD = 128


def on_device(queries, k_cache, v_cache, new_keys, new_values, fill, owner, out_weight):
    steps, batch = owner.shape
    rows = k_cache.shape[1]
    device_pos = lax.axis_index("ctx")
    mine = (owner == device_pos).astype(jnp.int32)
    seen = jnp.cumsum(mine, axis=0)
    local_fill = fill[:, 0]
    slot = local_fill[None, :] + seen - 1
    row_ids = lax.broadcasted_iota(jnp.int32, (batch, rows), 1)
    keys_out, values_out = (k_cache, v_cache)
    for step in range(steps):
        target = ((row_ids == slot[step][:, None]) & (mine[step][:, None] == 1))[:, :, None]
        keys_out = jnp.where(target, new_keys[step][:, None, :], keys_out)
        values_out = jnp.where(target, new_values[step][:, None, :], values_out)
    lengths = local_fill[None, :] + seen
    kv_local = keys_out.shape[2] // HD
    groups = queries.shape[2] // (kv_local * HD)
    query_heads = queries.reshape(steps, batch, kv_local, groups, HD)
    key_heads = keys_out.reshape(batch, rows, kv_local, HD)
    value_heads = values_out.reshape(batch, rows, kv_local, HD)
    scores = jnp.einsum(
        "sbgqd,brgd->sbgqr", query_heads, key_heads, preferred_element_type=jnp.float32
    ) * (1.0 / HD**0.5)
    slot_ids = lax.broadcasted_iota(jnp.int32, (1, 1, 1, 1, rows), 4)
    live = slot_ids < lengths[:, :, None, None, None]
    masked = jnp.where(live, scores, -1e30)
    peak = jnp.max(masked, axis=-1)
    weights = jnp.where(live, jnp.exp(masked - peak[..., None]), 0.0)
    total = jnp.sum(weights, axis=-1)
    rounded = weights.astype(jnp.bfloat16)
    numer = jnp.einsum(
        "sbgqr,brgd->sbgqd", rounded, value_heads, preferred_element_type=jnp.float32
    )
    largest = lax.pmax(peak, "ctx")
    factor = jnp.exp(peak - largest)
    numer_all, total_all = lax.psum((numer * factor[..., None], total * factor), "ctx")
    attention = (numer_all / total_all[..., None]).astype(jnp.bfloat16)
    attention_rows = attention.reshape(steps * batch, kv_local * groups * HD)
    partial_out = jnp.dot(attention_rows, out_weight, preferred_element_type=jnp.float32)
    mixed = lax.psum_scatter(partial_out, "head", scatter_dimension=1, tiled=True).astype(
        jnp.bfloat16
    )
    return (keys_out, values_out, mixed.reshape(steps, batch, -1))


MESH = pl.DeviceIdType.MESH
STAT_ROWS = 16
VMEM_BYTES = 64 * 1024 * 1024


def new_rows(old, slots, rows_f32, step_rows):
    ids = lax.broadcasted_iota(jnp.int32, old.shape, 0)
    out = old.astype(jnp.float32)
    for slot, row in zip(slots, step_rows):
        out = jnp.where(ids == slot, rows_f32[row : row + 1, :], out)
    return out.astype(old.dtype)


def fused_kernel(
    n_ctx, n_head, steps, batch, groups, kv_local,
    fill, owner, q_hbm, k_hbm, v_hbm, nk_hbm, nv_hbm, w_hbm,
    k_out, v_out, mixed,
    q_v, nk_v, nv_v, k_v, v_v, w_v, q_rows, part, stat, nk_f, nv_f,
    send1, recv1, send2, recv2, send3, recv3,
    small_sem, k_sem, v_sem, w_sem, ko_sem, vo_sem,
    ssem1, rsem1, ssem2, rsem2, ssem3, rsem3,
):
    me = lax.axis_index("ctx")
    hme = lax.axis_index("head")
    tokens = steps * batch
    rows = k_v.shape[1]
    heads = groups * kv_local
    per = heads // n_ctx
    block = per * tokens
    depth = per * HD
    width = mixed.shape[2]

    barrier = pltpu.get_barrier_semaphore()
    for d in range(1, n_ctx):
        pl.semaphore_signal(barrier, inc=1, device_id={"ctx": lax.rem(me + d, n_ctx)}, device_id_type=MESH)
    for d in range(1, n_head):
        pl.semaphore_signal(barrier, inc=1, device_id={"head": lax.rem(hme + d, n_head)}, device_id_type=MESH)

    smalls = [
        pltpu.make_async_copy(q_hbm, q_v, small_sem.at[0]),
        pltpu.make_async_copy(nk_hbm, nk_v, small_sem.at[1]),
        pltpu.make_async_copy(nv_hbm, nv_v, small_sem.at[2]),
    ]
    k_in = [pltpu.make_async_copy(k_hbm.at[b], k_v.at[b], k_sem.at[b]) for b in range(batch)]
    v_in = [pltpu.make_async_copy(v_hbm.at[b], v_v.at[b], v_sem.at[b]) for b in range(batch)]
    w_in = [
        pltpu.make_async_copy(w_hbm.at[pl.ds(c * depth, depth), :], w_v.at[c], w_sem.at[c])
        for c in range(n_ctx)
    ]
    for copy in smalls:
        copy.start()
    for b in range(batch):
        k_in[b].start()
        v_in[b].start()
    for copy in w_in:
        copy.start()

    smalls[0].wait()
    for s in range(steps):
        q_f = q_v[s].astype(jnp.float32)
        for h in range(heads):
            q_rows[h * tokens + s * batch : h * tokens + (s + 1) * batch, :] = q_f[:, h * HD : (h + 1) * HD]
    smalls[1].wait()
    smalls[2].wait()
    for s in range(steps):
        nk_f[s * batch : (s + 1) * batch, :] = nk_v[s].astype(jnp.float32)
        nv_f[s * batch : (s + 1) * batch, :] = nv_v[s].astype(jnp.float32)

    live_rows = groups * steps
    step_ids = lax.rem(lax.broadcasted_iota(jnp.int32, (live_rows, rows), 0), steps)
    slot_ids = lax.broadcasted_iota(jnp.int32, (live_rows, rows), 1)
    lane = lax.broadcasted_iota(jnp.int32, (live_rows, HD), 1)
    pick = (
        lax.broadcasted_iota(jnp.int32, (STAT_ROWS, HD), 0)
        == lax.broadcasted_iota(jnp.int32, (STAT_ROWS, HD), 1)
    ).astype(jnp.bfloat16)

    slots, lengths = [], []
    for b in range(batch):
        seen = fill[b]
        slots_b, lengths_b = [], []
        for s in range(steps):
            mine = owner[s, b] == me
            slots_b.append(jnp.where(mine, seen, -1))
            seen = seen + jnp.where(mine, 1, 0)
            lengths_b.append(seen)
        slots.append(slots_b)
        lengths.append(lengths_b)

    def first(c):
        d = lax.rem(c - me + n_ctx, n_ctx)
        return pltpu.make_async_remote_copy(
            src_ref=send1.at[c], dst_ref=recv1.at[d], send_sem=ssem1.at[c], recv_sem=rsem1.at[d],
            device_id={"ctx": c}, device_id_type=MESH,
        )

    for b in range(batch):
        k_in[b].wait()
    for b in range(batch):
        v_in[b].wait()
    all_b = range(batch)
    sent = 0
    for g in range(kv_local):
        cols = slice(g * HD, (g + 1) * HD)
        nk_g, nv_g = nk_f[:, cols], nv_f[:, cols]
        at = [pl.ds(g * groups * tokens + b, live_rows, stride=batch) for b in all_b]
        step_rows = [[s * batch + b for s in range(steps)] for b in all_b]
        query = [q_rows[at[b], :].astype(jnp.bfloat16) for b in all_b]
        keys = [new_rows(k_v[b, :, cols], slots[b], nk_g, step_rows[b]) for b in all_b]
        scores = [
            lax.dot_general(
                query[b], keys[b], (((1,), (1,)), ((), ())), preferred_element_type=jnp.float32
            )
            for b in all_b
        ]
        for b in all_b:
            k_v[b, :, cols] = keys[b]
        values = [new_rows(v_v[b, :, cols], slots[b], nv_g, step_rows[b]) for b in all_b]
        for b in all_b:
            v_v[b, :, cols] = values[b]
        live = []
        for b in all_b:
            length = jnp.full((live_rows, rows), lengths[b][steps - 1], jnp.int32)
            for s in range(steps - 1):
                length = jnp.where(step_ids == s, lengths[b][s], length)
            live.append(slot_ids < length)
        masked = [jnp.where(live[b], scores[b] * (1.0 / HD**0.5), -1e30) for b in all_b]
        peak = [jnp.max(masked[b], axis=1, keepdims=True) for b in all_b]
        weights = [jnp.where(live[b], jnp.exp(masked[b] - peak[b]), 0.0) for b in all_b]
        total = [jnp.sum(weights[b], axis=1, keepdims=True) for b in all_b]
        sums = [
            jnp.dot(
                weights[b].astype(jnp.bfloat16), values[b], preferred_element_type=jnp.float32
            )
            for b in all_b
        ]
        for b in all_b:
            part[at[b], :] = sums[b]
        for b in all_b:
            both = jnp.where(lax.rem(lane, 2) == 0, peak[b], total[b])
            high = both.astype(jnp.bfloat16).astype(jnp.float32)
            middle = (both - high).astype(jnp.bfloat16).astype(jnp.float32)
            low = both - high - middle
            stat[at[b], :] = jnp.where(lane < 2, high, jnp.where(lane < 4, middle, low))
        ready = n_ctx * (g + 1) // kv_local
        for c in range(sent, ready):
            here = slice(c * block, (c + 1) * block)
            send1[c, 0:block, :] = part[here, :].astype(jnp.bfloat16)
            turned = lax.dot_general(
                pick, stat[here, :].astype(jnp.bfloat16), (((1,), (1,)), ((), ())),
                preferred_element_type=jnp.float32,
            )
            send1[c, block : block + STAT_ROWS, 0:block] = turned.astype(jnp.bfloat16)
        if g == 0:
            pl.semaphore_wait(barrier, n_ctx + n_head - 2)
        for c in range(sent, ready):

            @pl.when(me != c)
            def _(c=c):
                first(c).start()

        sent = ready

    outs = [pltpu.make_async_copy(k_v.at[b], k_out.at[b], ko_sem.at[b]) for b in all_b]
    outs += [pltpu.make_async_copy(v_v.at[b], v_out.at[b], vo_sem.at[b]) for b in all_b]
    for copy in outs:
        copy.start()
    recv1[0] = send1[me]
    for d in range(1, n_ctx):
        pltpu.make_async_remote_copy(
            src_ref=send1.at[0], dst_ref=recv1.at[d], send_sem=ssem1.at[0], recv_sem=rsem1.at[d],
            device_id={"ctx": lax.rem(me + d, n_ctx)}, device_id_type=MESH,
        ).wait_recv()
    peaks, totals = [], []
    for d in range(n_ctx):
        got = recv1[d, block : block + STAT_ROWS, 0:block].astype(jnp.float32)
        peaks.append(got[0:1] + got[2:3] + got[4:5])
        totals.append(got[1:2] + got[3:4] + got[5:6])
    peaks = jnp.concatenate(peaks, axis=0)
    totals = jnp.concatenate(totals, axis=0)
    factor = jnp.exp(peaks - jnp.max(peaks, axis=0, keepdims=True))
    shares = factor / jnp.sum(factor * totals, axis=0, keepdims=True)
    shares = jnp.transpose(shares)
    attention = jnp.zeros((block, HD), jnp.float32)
    for d in range(n_ctx):
        attention += recv1[d, 0:block, :].astype(jnp.float32) * shares[:, d : d + 1]
    send2[...] = attention.astype(jnp.bfloat16)

    second = []
    for d in range(1, n_ctx):
        copy = pltpu.make_async_remote_copy(
            src_ref=send2, dst_ref=recv2.at[d], send_sem=ssem2.at[d], recv_sem=rsem2.at[d],
            device_id={"ctx": lax.rem(me + d, n_ctx)}, device_id_type=MESH,
        )
        copy.start()
        second.append(copy)
    for copy in w_in:
        copy.wait()
    share = None
    for d in range(n_ctx):
        if d > 0:
            second[d - 1].wait_recv()
            got = recv2[d].astype(jnp.float32)
        else:
            got = send2[...].astype(jnp.float32)
        features = jnp.concatenate(
            [got[i * tokens : (i + 1) * tokens] for i in range(per)], axis=1
        ).astype(jnp.bfloat16)
        product = jnp.dot(
            features, w_v[lax.rem(me - d + n_ctx, n_ctx)], preferred_element_type=jnp.float32
        )
        share = product if share is None else share + product
    for h in range(n_head):
        send3[h] = share[:, h * width : (h + 1) * width]
    third = []
    for d in range(1, n_head):
        target = lax.rem(hme + d, n_head)
        copy = pltpu.make_async_remote_copy(
            src_ref=send3.at[target], dst_ref=recv3.at[d], send_sem=ssem3.at[d], recv_sem=rsem3.at[d],
            device_id={"head": target}, device_id_type=MESH,
        )
        copy.start()
        third.append(copy)
    result = send3[hme]
    for copy in third:
        copy.wait_recv()
    for d in range(1, n_head):
        result += recv3[d]
    result = result.astype(mixed.dtype)
    for s in range(steps):
        mixed[s] = result[s * batch : (s + 1) * batch]

    for c in range(n_ctx):

        @pl.when(me != c)
        def _(c=c):
            first(c).wait_send()

    for copy in second:
        copy.wait_send()
    for copy in third:
        copy.wait_send()
    for copy in outs:
        copy.wait()


def on_device_fused(
    n_ctx, n_head, queries, k_cache, v_cache, new_keys, new_values, fill, owner, out_weight
):
    steps, batch, features = queries.shape
    rows, kv_width = k_cache.shape[1:]
    kv_local = kv_width // HD
    heads = features // HD
    tokens = steps * batch
    columns = out_weight.shape[1]
    per = heads // n_ctx
    block = per * tokens
    if heads % n_ctx or block % 16 or block > HD or n_ctx % kv_local or batch != 8 or columns % (n_head * HD):
        return on_device(
            queries, k_cache, v_cache, new_keys, new_values, fill, owner, out_weight
        )
    kernel = functools.partial(
        fused_kernel, n_ctx, n_head, steps, batch, heads // kv_local, kv_local
    )
    whole = pl.BlockSpec(memory_space=pl.ANY)
    scalars = pl.BlockSpec(memory_space=pltpu.SMEM)
    dma = pltpu.SemaphoreType.DMA
    return pl.pallas_call(
        kernel,
        out_shape=(
            jax.ShapeDtypeStruct(k_cache.shape, k_cache.dtype),
            jax.ShapeDtypeStruct(v_cache.shape, v_cache.dtype),
            jax.ShapeDtypeStruct((steps, batch, columns // n_head), jnp.bfloat16),
        ),
        in_specs=[scalars, scalars] + [whole] * 6,
        out_specs=(whole, whole, pl.BlockSpec(memory_space=pltpu.VMEM)),
        scratch_shapes=[
            pltpu.VMEM(queries.shape, jnp.bfloat16),
            pltpu.VMEM(new_keys.shape, jnp.bfloat16),
            pltpu.VMEM(new_values.shape, jnp.bfloat16),
            pltpu.VMEM(k_cache.shape, jnp.bfloat16),
            pltpu.VMEM(v_cache.shape, jnp.bfloat16),
            pltpu.VMEM((n_ctx, per * HD, columns), jnp.bfloat16),
            pltpu.VMEM((heads * tokens, HD), jnp.float32),
            pltpu.VMEM((heads * tokens, HD), jnp.float32),
            pltpu.VMEM((heads * tokens, HD), jnp.float32),
            pltpu.VMEM((tokens, kv_width), jnp.float32),
            pltpu.VMEM((tokens, kv_width), jnp.float32),
            pltpu.VMEM((n_ctx, block + STAT_ROWS, HD), jnp.bfloat16),
            pltpu.VMEM((n_ctx, block + STAT_ROWS, HD), jnp.bfloat16),
            pltpu.VMEM((block, HD), jnp.bfloat16),
            pltpu.VMEM((n_ctx, block, HD), jnp.bfloat16),
            pltpu.VMEM((n_head, tokens, columns // n_head), jnp.float32),
            pltpu.VMEM((n_head, tokens, columns // n_head), jnp.float32),
            dma((3,)),
            dma((batch,)),
            dma((batch,)),
            dma((n_ctx,)),
            dma((batch,)),
            dma((batch,)),
            dma((n_ctx,)),
            dma((n_ctx,)),
            dma((n_ctx,)),
            dma((n_ctx,)),
            dma((n_head,)),
            dma((n_head,)),
        ],
        compiler_params=pltpu.CompilerParams(
            collective_id=0, has_side_effects=True, vmem_limit_bytes=VMEM_BYTES
        ),
        cost_estimate=pl.CostEstimate(
            flops=2 * tokens * features * (columns + 2 * rows),
            bytes_accessed=2 * (2 * k_cache.size + 2 * v_cache.size + out_weight.size),
            transcendentals=tokens * heads * rows,
        ),
    )(fill.reshape(batch), owner, queries, k_cache, v_cache, new_keys, new_values, out_weight)


def solution(mesh):
    in_specs = (
        P(None, None, "head"),
        P(None, "ctx", "head"),
        P(None, "ctx", "head"),
        P(None, None, "head"),
        P(None, None, "head"),
        P(None, "ctx"),
        P(),
        P("head", "ctx"),
    )
    out_specs = (P(None, "ctx", "head"), P(None, "ctx", "head"), P(None, None, ("ctx", "head")))
    return jax.shard_map(
        functools.partial(on_device_fused, mesh.shape["ctx"], mesh.shape["head"]), mesh=mesh, in_specs=in_specs, out_specs=out_specs, check_vma=False
    )
```

```python
import functools

import jax
import jax.numpy as jnp
from jax import lax
from jax.experimental import pallas as pl
from jax.experimental.pallas import tpu as pltpu
from jax.sharding import PartitionSpec as P

HD = 128


def on_device(queries, k_cache, v_cache, new_keys, new_values, fill, owner, out_weight):
    steps, batch = owner.shape
    rows = k_cache.shape[1]
    device_pos = lax.axis_index("ctx")
    mine = (owner == device_pos).astype(jnp.int32)
    seen = jnp.cumsum(mine, axis=0)
    local_fill = fill[:, 0]
    slot = local_fill[None, :] + seen - 1
    row_ids = lax.broadcasted_iota(jnp.int32, (batch, rows), 1)
    keys_out, values_out = (k_cache, v_cache)
    for step in range(steps):
        target = ((row_ids == slot[step][:, None]) & (mine[step][:, None] == 1))[:, :, None]
        keys_out = jnp.where(target, new_keys[step][:, None, :], keys_out)
        values_out = jnp.where(target, new_values[step][:, None, :], values_out)
    lengths = local_fill[None, :] + seen
    kv_local = keys_out.shape[2] // HD
    groups = queries.shape[2] // (kv_local * HD)
    query_heads = queries.reshape(steps, batch, kv_local, groups, HD)
    key_heads = keys_out.reshape(batch, rows, kv_local, HD)
    value_heads = values_out.reshape(batch, rows, kv_local, HD)
    scores = jnp.einsum(
        "sbgqd,brgd->sbgqr", query_heads, key_heads, preferred_element_type=jnp.float32
    ) * (1.0 / HD**0.5)
    slot_ids = lax.broadcasted_iota(jnp.int32, (1, 1, 1, 1, rows), 4)
    live = slot_ids < lengths[:, :, None, None, None]
    masked = jnp.where(live, scores, -1e30)
    peak = jnp.max(masked, axis=-1)
    weights = jnp.where(live, jnp.exp(masked - peak[..., None]), 0.0)
    total = jnp.sum(weights, axis=-1)
    rounded = weights.astype(jnp.bfloat16)
    numer = jnp.einsum(
        "sbgqr,brgd->sbgqd", rounded, value_heads, preferred_element_type=jnp.float32
    )
    largest = lax.pmax(peak, "ctx")
    factor = jnp.exp(peak - largest)
    numer_all, total_all = lax.psum((numer * factor[..., None], total * factor), "ctx")
    attention = (numer_all / total_all[..., None]).astype(jnp.bfloat16)
    attention_rows = attention.reshape(steps * batch, kv_local * groups * HD)
    partial_out = jnp.dot(attention_rows, out_weight, preferred_element_type=jnp.float32)
    mixed = lax.psum_scatter(partial_out, "head", scatter_dimension=1, tiled=True).astype(
        jnp.bfloat16
    )
    return (keys_out, values_out, mixed.reshape(steps, batch, -1))


MESH = pl.DeviceIdType.MESH
STAT_ROWS = 16
VMEM_BYTES = 32 * 1024 * 1024


def new_rows(old, slots, rows_f32, step_rows):
    ids = lax.broadcasted_iota(jnp.int32, old.shape, 0)
    out = old.astype(jnp.float32)
    for slot, row in zip(slots, step_rows):
        out = jnp.where(ids == slot, rows_f32[row : row + 1, :], out)
    return out.astype(old.dtype)


def fused_kernel(
    n_ctx, n_head, steps, batch, groups, kv_local,
    fill_hbm, owner_hbm, q_hbm, k_hbm, v_hbm, nk_hbm, nv_hbm, w_hbm,
    k_out, v_out, mixed,
    fill, owner, q_v, nk_v, nv_v, k_v, v_v, w_v, q_rows, part, stat, nk_f, nv_f,
    send1, recv1, send2, recv2, send3, recv3,
    small_sem, k_sem, v_sem, w_sem, ko_sem, vo_sem,
    ssem1, rsem1, ssem2, rsem2, ssem3, rsem3,
):
    me = lax.axis_index("ctx")
    hme = lax.axis_index("head")
    tokens = steps * batch
    rows = k_v.shape[1]
    heads = groups * kv_local
    per = heads // n_ctx
    block = per * tokens
    depth = per * HD
    width = mixed.shape[2]

    barrier = pltpu.get_barrier_semaphore()
    for d in range(1, n_ctx):
        pl.semaphore_signal(barrier, inc=1, device_id={"ctx": lax.rem(me + d, n_ctx)}, device_id_type=MESH)
    for d in range(1, n_head):
        pl.semaphore_signal(barrier, inc=1, device_id={"head": lax.rem(hme + d, n_head)}, device_id_type=MESH)

    smalls = [
        pltpu.make_async_copy(q_hbm, q_v, small_sem.at[0]),
        pltpu.make_async_copy(nk_hbm, nk_v, small_sem.at[1]),
        pltpu.make_async_copy(nv_hbm, nv_v, small_sem.at[2]),
        pltpu.make_async_copy(fill_hbm, fill, small_sem.at[3]),
        pltpu.make_async_copy(owner_hbm, owner, small_sem.at[4]),
    ]
    k_in = [pltpu.make_async_copy(k_hbm.at[b], k_v.at[b], k_sem.at[b]) for b in range(batch)]
    v_in = [pltpu.make_async_copy(v_hbm.at[b], v_v.at[b], v_sem.at[b]) for b in range(batch)]
    w_in = [
        pltpu.make_async_copy(w_hbm.at[pl.ds(c * depth, depth), :], w_v.at[c], w_sem.at[c])
        for c in range(n_ctx)
    ]
    for copy in smalls:
        copy.start()
    for b in range(batch):
        k_in[b].start()
        v_in[b].start()
    for copy in w_in:
        copy.start()

    smalls[0].wait()
    for s in range(steps):
        q_f = q_v[s].astype(jnp.float32)
        for h in range(heads):
            q_rows[h * tokens + s * batch : h * tokens + (s + 1) * batch, :] = q_f[:, h * HD : (h + 1) * HD]
    smalls[1].wait()
    smalls[2].wait()
    for s in range(steps):
        nk_f[s * batch : (s + 1) * batch, :] = nk_v[s].astype(jnp.float32)
        nv_f[s * batch : (s + 1) * batch, :] = nv_v[s].astype(jnp.float32)

    live_rows = groups * steps
    step_ids = lax.rem(lax.broadcasted_iota(jnp.int32, (live_rows, rows), 0), steps)
    slot_ids = lax.broadcasted_iota(jnp.int32, (live_rows, rows), 1)
    lane = lax.broadcasted_iota(jnp.int32, (live_rows, HD), 1)
    pick = (
        lax.broadcasted_iota(jnp.int32, (STAT_ROWS, HD), 0)
        == lax.broadcasted_iota(jnp.int32, (STAT_ROWS, HD), 1)
    ).astype(jnp.bfloat16)

    smalls[3].wait()
    smalls[4].wait()
    slots, lengths = [], []
    for b in range(batch):
        seen = fill[b]
        slots_b, lengths_b = [], []
        for s in range(steps):
            mine = owner[s, b] == me
            slots_b.append(jnp.where(mine, seen, -1))
            seen = seen + jnp.where(mine, 1, 0)
            lengths_b.append(seen)
        slots.append(slots_b)
        lengths.append(lengths_b)

    def first(c):
        d = lax.rem(c - me + n_ctx, n_ctx)
        return pltpu.make_async_remote_copy(
            src_ref=send1.at[c], dst_ref=recv1.at[d], send_sem=ssem1.at[c], recv_sem=rsem1.at[d],
            device_id={"ctx": c}, device_id_type=MESH,
        )

    for b in range(batch):
        k_in[b].wait()
    for b in range(batch):
        v_in[b].wait()
    all_b = range(batch)
    sent = 0
    for g in range(kv_local):
        cols = slice(g * HD, (g + 1) * HD)
        nk_g, nv_g = nk_f[:, cols], nv_f[:, cols]
        at = [pl.ds(g * groups * tokens + b, live_rows, stride=batch) for b in all_b]
        step_rows = [[s * batch + b for s in range(steps)] for b in all_b]
        query = [q_rows[at[b], :].astype(jnp.bfloat16) for b in all_b]
        keys = [new_rows(k_v[b, :, cols], slots[b], nk_g, step_rows[b]) for b in all_b]
        scores = [
            lax.dot_general(
                query[b], keys[b], (((1,), (1,)), ((), ())), preferred_element_type=jnp.float32
            )
            for b in all_b
        ]
        for b in all_b:
            k_v[b, :, cols] = keys[b]
        values = [new_rows(v_v[b, :, cols], slots[b], nv_g, step_rows[b]) for b in all_b]
        for b in all_b:
            v_v[b, :, cols] = values[b]
        live = []
        for b in all_b:
            length = jnp.full((live_rows, rows), lengths[b][steps - 1], jnp.int32)
            for s in range(steps - 1):
                length = jnp.where(step_ids == s, lengths[b][s], length)
            live.append(slot_ids < length)
        masked = [jnp.where(live[b], scores[b] * (1.0 / HD**0.5), -1e30) for b in all_b]
        peak = [jnp.max(masked[b], axis=1, keepdims=True) for b in all_b]
        weights = [jnp.where(live[b], jnp.exp(masked[b] - peak[b]), 0.0) for b in all_b]
        total = [jnp.sum(weights[b], axis=1, keepdims=True) for b in all_b]
        sums = [
            jnp.dot(
                weights[b].astype(jnp.bfloat16), values[b], preferred_element_type=jnp.float32
            )
            for b in all_b
        ]
        for b in all_b:
            part[at[b], :] = sums[b]
        for b in all_b:
            both = jnp.where(lax.rem(lane, 2) == 0, peak[b], total[b])
            high = both.astype(jnp.bfloat16).astype(jnp.float32)
            middle = (both - high).astype(jnp.bfloat16).astype(jnp.float32)
            low = both - high - middle
            stat[at[b], :] = jnp.where(lane < 2, high, jnp.where(lane < 4, middle, low))
        ready = n_ctx * (g + 1) // kv_local
        for c in range(sent, ready):
            here = slice(c * block, (c + 1) * block)
            send1[c, 0:block, :] = part[here, :].astype(jnp.bfloat16)
            turned = lax.dot_general(
                pick, stat[here, :].astype(jnp.bfloat16), (((1,), (1,)), ((), ())),
                preferred_element_type=jnp.float32,
            )
            send1[c, block : block + STAT_ROWS, 0:block] = turned.astype(jnp.bfloat16)
        if g == 0:
            pl.semaphore_wait(barrier, n_ctx + n_head - 2)
        for c in range(sent, ready):

            @pl.when(me != c)
            def _(c=c):
                first(c).start()

        sent = ready

    outs = [pltpu.make_async_copy(k_v.at[b], k_out.at[b], ko_sem.at[b]) for b in all_b]
    outs += [pltpu.make_async_copy(v_v.at[b], v_out.at[b], vo_sem.at[b]) for b in all_b]
    for copy in outs:
        copy.start()
    recv1[0] = send1[me]
    for d in range(1, n_ctx):
        pltpu.make_async_remote_copy(
            src_ref=send1.at[0], dst_ref=recv1.at[d], send_sem=ssem1.at[0], recv_sem=rsem1.at[d],
            device_id={"ctx": lax.rem(me + d, n_ctx)}, device_id_type=MESH,
        ).wait_recv()
    peaks, totals = [], []
    for d in range(n_ctx):
        got = recv1[d, block : block + STAT_ROWS, 0:block].astype(jnp.float32)
        peaks.append(got[0:1] + got[2:3] + got[4:5])
        totals.append(got[1:2] + got[3:4] + got[5:6])
    peaks = jnp.concatenate(peaks, axis=0)
    totals = jnp.concatenate(totals, axis=0)
    factor = jnp.exp(peaks - jnp.max(peaks, axis=0, keepdims=True))
    shares = factor / jnp.sum(factor * totals, axis=0, keepdims=True)
    shares = jnp.transpose(shares)
    attention = jnp.zeros((block, HD), jnp.float32)
    for d in range(n_ctx):
        attention += recv1[d, 0:block, :].astype(jnp.float32) * shares[:, d : d + 1]
    send2[...] = attention.astype(jnp.bfloat16)

    second = []
    for d in range(1, n_ctx):
        copy = pltpu.make_async_remote_copy(
            src_ref=send2, dst_ref=recv2.at[d], send_sem=ssem2.at[d], recv_sem=rsem2.at[d],
            device_id={"ctx": lax.rem(me + d, n_ctx)}, device_id_type=MESH,
        )
        copy.start()
        second.append(copy)
    for copy in w_in:
        copy.wait()
    share = None
    for d in range(n_ctx):
        if d > 0:
            second[d - 1].wait_recv()
            got = recv2[d].astype(jnp.float32)
        else:
            got = send2[...].astype(jnp.float32)
        features = jnp.concatenate(
            [got[i * tokens : (i + 1) * tokens] for i in range(per)], axis=1
        ).astype(jnp.bfloat16)
        product = jnp.dot(
            features, w_v[lax.rem(me - d + n_ctx, n_ctx)], preferred_element_type=jnp.float32
        )
        share = product if share is None else share + product
    for h in range(n_head):
        send3[h] = share[:, h * width : (h + 1) * width]
    third = []
    for d in range(1, n_head):
        target = lax.rem(hme + d, n_head)
        copy = pltpu.make_async_remote_copy(
            src_ref=send3.at[target], dst_ref=recv3.at[d], send_sem=ssem3.at[d], recv_sem=rsem3.at[d],
            device_id={"head": target}, device_id_type=MESH,
        )
        copy.start()
        third.append(copy)
    result = send3[hme]
    for copy in third:
        copy.wait_recv()
    for d in range(1, n_head):
        result += recv3[d]
    result = result.astype(mixed.dtype)
    for s in range(steps):
        mixed[s] = result[s * batch : (s + 1) * batch]

    for c in range(n_ctx):

        @pl.when(me != c)
        def _(c=c):
            first(c).wait_send()

    for copy in second:
        copy.wait_send()
    for copy in third:
        copy.wait_send()
    for copy in outs:
        copy.wait()


def write_kernel(k_in, v_in, m_in, k_out, v_out, m_out, sems):
    batch = k_in.shape[0]
    copies = [pltpu.make_async_copy(m_in, m_out, sems.at[2 * batch])]
    for b in range(batch):
        copies.append(pltpu.make_async_copy(k_in.at[b], k_out.at[b], sems.at[b]))
        copies.append(pltpu.make_async_copy(v_in.at[b], v_out.at[b], sems.at[batch + b]))
    for copy in copies:
        copy.start()
    for copy in copies:
        copy.wait()


def on_device_fused(
    n_ctx, n_head, queries, k_cache, v_cache, new_keys, new_values, fill, owner, out_weight
):
    steps, batch, features = queries.shape
    rows, kv_width = k_cache.shape[1:]
    kv_local = kv_width // HD
    heads = features // HD
    tokens = steps * batch
    columns = out_weight.shape[1]
    per = heads // n_ctx
    block = per * tokens
    if heads % n_ctx or block % 16 or block > HD or n_ctx % kv_local or batch != 8 or columns % (n_head * HD):
        return on_device(
            queries, k_cache, v_cache, new_keys, new_values, fill, owner, out_weight
        )
    kernel = functools.partial(
        fused_kernel, n_ctx, n_head, steps, batch, heads // kv_local, kv_local
    )
    whole = pl.BlockSpec(memory_space=pl.ANY)
    dma = pltpu.SemaphoreType.DMA
    shapes = (
        jax.ShapeDtypeStruct(k_cache.shape, k_cache.dtype),
        jax.ShapeDtypeStruct(v_cache.shape, v_cache.dtype),
        jax.ShapeDtypeStruct((steps, batch, columns // n_head), jnp.bfloat16),
    )
    results = pl.pallas_call(
        kernel,
        out_shape=shapes,
        in_specs=[whole] * 8,
        out_specs=(whole, whole, pl.BlockSpec(memory_space=pltpu.VMEM)),
        scratch_shapes=[
            pltpu.SMEM((batch,), jnp.int32),
            pltpu.SMEM((steps, batch), jnp.int32),
            pltpu.VMEM(queries.shape, jnp.bfloat16),
            pltpu.VMEM(new_keys.shape, jnp.bfloat16),
            pltpu.VMEM(new_values.shape, jnp.bfloat16),
            pltpu.VMEM(k_cache.shape, jnp.bfloat16),
            pltpu.VMEM(v_cache.shape, jnp.bfloat16),
            pltpu.VMEM((n_ctx, per * HD, columns), jnp.bfloat16),
            pltpu.VMEM((heads * tokens, HD), jnp.float32),
            pltpu.VMEM((heads * tokens, HD), jnp.float32),
            pltpu.VMEM((heads * tokens, HD), jnp.float32),
            pltpu.VMEM((tokens, kv_width), jnp.float32),
            pltpu.VMEM((tokens, kv_width), jnp.float32),
            pltpu.VMEM((n_ctx, block + STAT_ROWS, HD), jnp.bfloat16),
            pltpu.VMEM((n_ctx, block + STAT_ROWS, HD), jnp.bfloat16),
            pltpu.VMEM((block, HD), jnp.bfloat16),
            pltpu.VMEM((n_ctx, block, HD), jnp.bfloat16),
            pltpu.VMEM((n_head, tokens, columns // n_head), jnp.float32),
            pltpu.VMEM((n_head, tokens, columns // n_head), jnp.float32),
            dma((5,)),
            dma((batch,)),
            dma((batch,)),
            dma((n_ctx,)),
            dma((batch,)),
            dma((batch,)),
            dma((n_ctx,)),
            dma((n_ctx,)),
            dma((n_ctx,)),
            dma((n_ctx,)),
            dma((n_head,)),
            dma((n_head,)),
        ],
        compiler_params=pltpu.CompilerParams(
            collective_id=0, has_side_effects=True, vmem_limit_bytes=VMEM_BYTES
        ),
        cost_estimate=pl.CostEstimate(
            flops=2 * tokens * features * (columns + 2 * rows),
            bytes_accessed=2 * (2 * k_cache.size + 2 * v_cache.size + out_weight.size),
            transcendentals=tokens * heads * rows,
        ),
    )(*[
        pltpu.with_memory_space_constraint(x, pltpu.HBM)
        for x in (
            fill.reshape(batch), owner, queries, k_cache, v_cache, new_keys, new_values, out_weight
        )
    ])
    return pl.pallas_call(
        write_kernel,
        out_shape=shapes,
        in_specs=[whole] * 3,
        out_specs=(whole,) * 3,
        scratch_shapes=[dma((2 * batch + 1,))],
        compiler_params=pltpu.CompilerParams(vmem_limit_bytes=1024 * 1024),
    )(*[pltpu.with_memory_space_constraint(x, pltpu.VMEM) for x in results])


def solution(mesh):
    in_specs = (
        P(None, None, "head"),
        P(None, "ctx", "head"),
        P(None, "ctx", "head"),
        P(None, None, "head"),
        P(None, None, "head"),
        P(None, "ctx"),
        P(),
        P("head", "ctx"),
    )
    out_specs = (P(None, "ctx", "head"), P(None, "ctx", "head"), P(None, None, ("ctx", "head")))
    return jax.shard_map(
        functools.partial(on_device_fused, mesh.shape["ctx"], mesh.shape["head"]), mesh=mesh, in_specs=in_specs, out_specs=out_specs, check_vma=False
    )
```

```python
import functools

import jax
import jax.numpy as jnp
from jax import lax
from jax.experimental import pallas as pl
from jax.experimental.pallas import tpu as pltpu
from jax.sharding import PartitionSpec as P

HD = 128


def on_device(queries, k_cache, v_cache, new_keys, new_values, fill, owner, out_weight):
    steps, batch = owner.shape
    rows = k_cache.shape[1]
    device_pos = lax.axis_index("ctx")
    mine = (owner == device_pos).astype(jnp.int32)
    seen = jnp.cumsum(mine, axis=0)
    local_fill = fill[:, 0]
    slot = local_fill[None, :] + seen - 1
    row_ids = lax.broadcasted_iota(jnp.int32, (batch, rows), 1)
    keys_out, values_out = (k_cache, v_cache)
    for step in range(steps):
        target = ((row_ids == slot[step][:, None]) & (mine[step][:, None] == 1))[:, :, None]
        keys_out = jnp.where(target, new_keys[step][:, None, :], keys_out)
        values_out = jnp.where(target, new_values[step][:, None, :], values_out)
    lengths = local_fill[None, :] + seen
    kv_local = keys_out.shape[2] // HD
    groups = queries.shape[2] // (kv_local * HD)
    query_heads = queries.reshape(steps, batch, kv_local, groups, HD)
    key_heads = keys_out.reshape(batch, rows, kv_local, HD)
    value_heads = values_out.reshape(batch, rows, kv_local, HD)
    scores = jnp.einsum(
        "sbgqd,brgd->sbgqr", query_heads, key_heads, preferred_element_type=jnp.float32
    ) * (1.0 / HD**0.5)
    slot_ids = lax.broadcasted_iota(jnp.int32, (1, 1, 1, 1, rows), 4)
    live = slot_ids < lengths[:, :, None, None, None]
    masked = jnp.where(live, scores, -1e30)
    peak = jnp.max(masked, axis=-1)
    weights = jnp.where(live, jnp.exp(masked - peak[..., None]), 0.0)
    total = jnp.sum(weights, axis=-1)
    rounded = weights.astype(jnp.bfloat16)
    numer = jnp.einsum(
        "sbgqr,brgd->sbgqd", rounded, value_heads, preferred_element_type=jnp.float32
    )
    largest = lax.pmax(peak, "ctx")
    factor = jnp.exp(peak - largest)
    numer_all, total_all = lax.psum((numer * factor[..., None], total * factor), "ctx")
    attention = (numer_all / total_all[..., None]).astype(jnp.bfloat16)
    attention_rows = attention.reshape(steps * batch, kv_local * groups * HD)
    partial_out = jnp.dot(attention_rows, out_weight, preferred_element_type=jnp.float32)
    mixed = lax.psum_scatter(partial_out, "head", scatter_dimension=1, tiled=True).astype(
        jnp.bfloat16
    )
    return (keys_out, values_out, mixed.reshape(steps, batch, -1))


MESH = pl.DeviceIdType.MESH
STAT_ROWS = 16
VMEM_BYTES = 32 * 1024 * 1024


def new_rows(old, slots, rows_f32, step_rows):
    ids = lax.broadcasted_iota(jnp.int32, old.shape, 0)
    out = old.astype(jnp.float32)
    for slot, row in zip(slots, step_rows):
        out = jnp.where(ids == slot, rows_f32[row : row + 1, :], out)
    return out.astype(old.dtype)


def fused_kernel(
    n_ctx, n_head, steps, batch, groups, kv_local,
    fill_hbm, owner_hbm, q_hbm, k_hbm, v_hbm, nk_hbm, nv_hbm, w_hbm,
    k_out, v_out, mixed,
    fill, owner, q_v, nk_v, nv_v, k_v, v_v, w_v, q_rows, part, stat, nk_f, nv_f,
    send1, recv1, send2, recv2, send3, recv3,
    small_sem, k_sem, v_sem, w_sem, ko_sem, vo_sem,
    ssem1, rsem1, ssem2, rsem2, ssem3, rsem3,
):
    me = lax.axis_index("ctx")
    hme = lax.axis_index("head")
    tokens = steps * batch
    rows = k_v.shape[1]
    heads = groups * kv_local
    per = heads // n_ctx
    block = per * tokens
    depth = per * HD
    width = mixed.shape[2]

    smalls = [
        pltpu.make_async_copy(q_hbm, q_v, small_sem.at[0]),
        pltpu.make_async_copy(nk_hbm, nk_v, small_sem.at[1]),
        pltpu.make_async_copy(nv_hbm, nv_v, small_sem.at[2]),
        pltpu.make_async_copy(fill_hbm, fill, small_sem.at[3]),
        pltpu.make_async_copy(owner_hbm, owner, small_sem.at[4]),
    ]
    k_in = [pltpu.make_async_copy(k_hbm.at[b], k_v.at[b], k_sem.at[b]) for b in range(batch)]
    v_in = [pltpu.make_async_copy(v_hbm.at[b], v_v.at[b], v_sem.at[b]) for b in range(batch)]
    w_in = [
        pltpu.make_async_copy(w_hbm.at[pl.ds(c * depth, depth), :], w_v.at[c], w_sem.at[c])
        for c in range(n_ctx)
    ]
    smalls[0].start()
    for copy in k_in:
        copy.start()
    for copy in smalls[1:]:
        copy.start()
    for copy in v_in:
        copy.start()

    barrier = pltpu.get_barrier_semaphore()
    for d in range(1, n_ctx):
        pl.semaphore_signal(barrier, inc=1, device_id={"ctx": lax.rem(me + d, n_ctx)}, device_id_type=MESH)
    for d in range(1, n_head):
        pl.semaphore_signal(barrier, inc=1, device_id={"head": lax.rem(hme + d, n_head)}, device_id_type=MESH)

    smalls[0].wait()
    for s in range(steps):
        q_f = q_v[s].astype(jnp.float32)
        for h in range(heads):
            q_rows[h * tokens + s * batch : h * tokens + (s + 1) * batch, :] = q_f[:, h * HD : (h + 1) * HD]
    smalls[1].wait()
    smalls[2].wait()
    nk_f[...] = jnp.zeros_like(nk_f)
    nv_f[...] = jnp.zeros_like(nv_f)
    for s in range(steps):
        nk_f[s * batch : (s + 1) * batch, :] = nk_v[s].astype(jnp.float32)
        nv_f[s * batch : (s + 1) * batch, :] = nv_v[s].astype(jnp.float32)

    live_rows = groups * steps
    slot_ids = lax.broadcasted_iota(jnp.int32, (live_rows, rows), 1)
    lane = lax.broadcasted_iota(jnp.int32, (live_rows, HD), 1)
    even = lax.rem(lane, 2) == 0
    step_ids = lax.rem(lax.broadcasted_iota(jnp.int32, (live_rows, HD), 0), steps)
    pick = (
        lax.broadcasted_iota(jnp.int32, (STAT_ROWS, HD), 0)
        == lax.broadcasted_iota(jnp.int32, (STAT_ROWS, HD), 1)
    ).astype(jnp.bfloat16)

    smalls[3].wait()
    smalls[4].wait()
    slots = []
    mine_ids = jnp.full((live_rows, HD), steps, jnp.int32)
    for b in range(batch):
        seen = fill[b]
        slots_b = []
        for s in range(steps):
            mine = owner[s, b] == me
            slots_b.append(jnp.where(mine, seen, -1))
            seen = seen + jnp.where(mine, 1, 0)
            mine_ids = jnp.where(lane == s * batch + b, jnp.where(mine, s, steps), mine_ids)
        slots.append(slots_b)
    visible = mine_ids <= step_ids
    new_live = [visible & (lax.rem(lane, batch) == b) for b in range(batch)]

    def first(c):
        d = lax.rem(c - me + n_ctx, n_ctx)
        return pltpu.make_async_remote_copy(
            src_ref=send1.at[c], dst_ref=recv1.at[d], send_sem=ssem1.at[c], recv_sem=rsem1.at[d],
            device_id={"ctx": c}, device_id_type=MESH,
        )

    all_b = range(batch)
    sent = 0
    for g in range(kv_local):
        cols = slice(g * HD, (g + 1) * HD)
        nk_g = nk_f[:, cols].astype(jnp.bfloat16)
        nv_g = nv_f[:, cols].astype(jnp.bfloat16)
        at = [pl.ds(g * groups * tokens + b, live_rows, stride=batch) for b in all_b]
        query = [q_rows[at[b], :].astype(jnp.bfloat16) for b in all_b]
        if g == 0:
            for copy in k_in:
                copy.wait()
        scores = [
            lax.dot_general(
                query[b], k_v[b, :, cols], (((1,), (1,)), ((), ())),
                preferred_element_type=jnp.float32,
            )
            for b in all_b
        ]
        new_scores = [
            lax.dot_general(
                query[b], nk_g, (((1,), (1,)), ((), ())), preferred_element_type=jnp.float32
            )
            for b in all_b
        ]
        masked = [
            jnp.where(slot_ids < fill[b], scores[b] * (1.0 / HD**0.5), -1e30) for b in all_b
        ]
        new_masked = [
            jnp.where(new_live[b], new_scores[b] * (1.0 / HD**0.5), -1e30) for b in all_b
        ]
        peak = [
            jnp.maximum(
                jnp.max(masked[b], axis=1, keepdims=True),
                jnp.max(new_masked[b], axis=1, keepdims=True),
            )
            for b in all_b
        ]
        weights = [jnp.exp(masked[b] - peak[b]) for b in all_b]
        new_weights = [jnp.exp(new_masked[b] - peak[b]) for b in all_b]
        total = [
            jnp.sum(weights[b], axis=1, keepdims=True)
            + jnp.sum(new_weights[b], axis=1, keepdims=True)
            for b in all_b
        ]
        if g == 0:
            for copy in v_in:
                copy.wait()
            for copy in w_in:
                copy.start()
        sums = [
            jnp.dot(
                weights[b].astype(jnp.bfloat16), v_v[b, :, cols],
                preferred_element_type=jnp.float32,
            )
            + jnp.dot(
                new_weights[b].astype(jnp.bfloat16), nv_g, preferred_element_type=jnp.float32
            )
            for b in all_b
        ]
        for b in all_b:
            part[at[b], :] = sums[b]
        for b in all_b:
            both = jnp.where(even, peak[b], total[b])
            high = both.astype(jnp.bfloat16).astype(jnp.float32)
            middle = (both - high).astype(jnp.bfloat16).astype(jnp.float32)
            low = both - high - middle
            stat[at[b], :] = jnp.where(lane < 2, high, jnp.where(lane < 4, middle, low))
        ready = n_ctx * (g + 1) // kv_local
        for c in range(sent, ready):
            here = slice(c * block, (c + 1) * block)
            send1[c, 0:block, :] = part[here, :].astype(jnp.bfloat16)
            turned = lax.dot_general(
                pick, stat[here, :].astype(jnp.bfloat16), (((1,), (1,)), ((), ())),
                preferred_element_type=jnp.float32,
            )
            send1[c, block : block + STAT_ROWS, 0:block] = turned.astype(jnp.bfloat16)
        if g == 0:
            pl.semaphore_wait(barrier, n_ctx + n_head - 2)
        for c in range(sent, ready):

            @pl.when(me != c)
            def _(c=c):
                first(c).start()

        sent = ready

    outs = [pltpu.make_async_copy(k_v.at[b], k_out.at[b], ko_sem.at[b]) for b in all_b]
    outs += [pltpu.make_async_copy(v_v.at[b], v_out.at[b], vo_sem.at[b]) for b in all_b]
    for b in all_b:
        step_rows = [s * batch + b for s in range(steps)]
        k_v[b] = new_rows(k_v[b], slots[b], nk_f, step_rows)
        v_v[b] = new_rows(v_v[b], slots[b], nv_f, step_rows)
    for copy in outs:
        copy.start()

    recv1[0] = send1[me]
    for d in range(1, n_ctx):
        pltpu.make_async_remote_copy(
            src_ref=send1.at[0], dst_ref=recv1.at[d], send_sem=ssem1.at[0], recv_sem=rsem1.at[d],
            device_id={"ctx": lax.rem(me + d, n_ctx)}, device_id_type=MESH,
        ).wait_recv()
    peaks, totals = [], []
    for d in range(n_ctx):
        got = recv1[d, block : block + STAT_ROWS, 0:block].astype(jnp.float32)
        peaks.append(got[0:1] + got[2:3] + got[4:5])
        totals.append(got[1:2] + got[3:4] + got[5:6])
    peaks = jnp.concatenate(peaks, axis=0)
    totals = jnp.concatenate(totals, axis=0)
    factor = jnp.exp(peaks - jnp.max(peaks, axis=0, keepdims=True))
    shares = factor / jnp.sum(factor * totals, axis=0, keepdims=True)
    shares = jnp.transpose(shares)
    attention = jnp.zeros((block, HD), jnp.float32)
    for d in range(n_ctx):
        attention += recv1[d, 0:block, :].astype(jnp.float32) * shares[:, d : d + 1]
    send2[...] = attention.astype(jnp.bfloat16)

    seconds = {}
    for d in sorted(range(1, n_ctx), key=lambda d: -min(d, n_ctx - d)):
        seconds[d] = pltpu.make_async_remote_copy(
            src_ref=send2, dst_ref=recv2.at[d], send_sem=ssem2.at[d], recv_sem=rsem2.at[d],
            device_id={"ctx": lax.rem(me + d, n_ctx)}, device_id_type=MESH,
        )
        seconds[d].start()
    for copy in w_in:
        copy.wait()
    order = [0] + sorted(range(1, n_ctx), key=lambda d: min(d, n_ctx - d))
    share = None
    for d in order:
        if d > 0:
            seconds[d].wait_recv()
            got = recv2[d].astype(jnp.float32)
        else:
            got = send2[...].astype(jnp.float32)
        features = jnp.concatenate(
            [got[i * tokens : (i + 1) * tokens] for i in range(per)], axis=1
        ).astype(jnp.bfloat16)
        source = lax.rem(me - d + n_ctx, n_ctx)
        if d == order[-1]:
            break
        product = jnp.dot(features, w_v[source], preferred_element_type=jnp.float32)
        share = product if share is None else share + product
    for h in range(n_head):
        send3[h] = share[:, h * width : (h + 1) * width]
    third = []
    for d in sorted(range(n_head), key=lambda d: -min(d, n_head - d)):
        target = lax.rem(hme + d, n_head)
        columns = pl.ds(pl.multiple_of(target * width, width), width)
        send3[target] = send3[target] + jnp.dot(
            features, w_v[source, :, columns], preferred_element_type=jnp.float32
        )
        if d > 0:
            copy = pltpu.make_async_remote_copy(
                src_ref=send3.at[target], dst_ref=recv3.at[d], send_sem=ssem3.at[d], recv_sem=rsem3.at[d],
                device_id={"head": target}, device_id_type=MESH,
            )
            copy.start()
            third.append(copy)
    result = send3[hme]
    for copy in third:
        copy.wait_recv()
    for d in range(1, n_head):
        result += recv3[d]
    result = result.astype(mixed.dtype)
    for s in range(steps):
        mixed[s] = result[s * batch : (s + 1) * batch]

    for c in range(n_ctx):

        @pl.when(me != c)
        def _(c=c):
            first(c).wait_send()

    for copy in seconds.values():
        copy.wait_send()
    for copy in third:
        copy.wait_send()
    for copy in outs:
        copy.wait()


def write_kernel(k_in, v_in, m_in, k_out, v_out, m_out, sems):
    batch = k_in.shape[0]
    copies = [pltpu.make_async_copy(m_in, m_out, sems.at[2 * batch])]
    for b in range(batch):
        copies.append(pltpu.make_async_copy(k_in.at[b], k_out.at[b], sems.at[b]))
        copies.append(pltpu.make_async_copy(v_in.at[b], v_out.at[b], sems.at[batch + b]))
    for copy in copies:
        copy.start()
    for copy in copies:
        copy.wait()


def on_device_fused(
    n_ctx, n_head, queries, k_cache, v_cache, new_keys, new_values, fill, owner, out_weight
):
    steps, batch, features = queries.shape
    rows, kv_width = k_cache.shape[1:]
    kv_local = kv_width // HD
    heads = features // HD
    tokens = steps * batch
    columns = out_weight.shape[1]
    per = heads // n_ctx
    block = per * tokens
    if heads % n_ctx or block % 16 or block > HD or n_ctx % kv_local or batch != 8 or tokens > HD or columns % (n_head * HD):
        return on_device(
            queries, k_cache, v_cache, new_keys, new_values, fill, owner, out_weight
        )
    kernel = functools.partial(
        fused_kernel, n_ctx, n_head, steps, batch, heads // kv_local, kv_local
    )
    whole = pl.BlockSpec(memory_space=pl.ANY)
    dma = pltpu.SemaphoreType.DMA
    shapes = (
        jax.ShapeDtypeStruct(k_cache.shape, k_cache.dtype),
        jax.ShapeDtypeStruct(v_cache.shape, v_cache.dtype),
        jax.ShapeDtypeStruct((steps, batch, columns // n_head), jnp.bfloat16),
    )
    results = pl.pallas_call(
        kernel,
        out_shape=shapes,
        in_specs=[whole] * 8,
        out_specs=(whole, whole, pl.BlockSpec(memory_space=pltpu.VMEM)),
        scratch_shapes=[
            pltpu.SMEM((batch,), jnp.int32),
            pltpu.SMEM((steps, batch), jnp.int32),
            pltpu.VMEM(queries.shape, jnp.bfloat16),
            pltpu.VMEM(new_keys.shape, jnp.bfloat16),
            pltpu.VMEM(new_values.shape, jnp.bfloat16),
            pltpu.VMEM(k_cache.shape, jnp.bfloat16),
            pltpu.VMEM(v_cache.shape, jnp.bfloat16),
            pltpu.VMEM((n_ctx, per * HD, columns), jnp.bfloat16),
            pltpu.VMEM((heads * tokens, HD), jnp.float32),
            pltpu.VMEM((heads * tokens, HD), jnp.float32),
            pltpu.VMEM((heads * tokens, HD), jnp.float32),
            pltpu.VMEM((HD, kv_width), jnp.float32),
            pltpu.VMEM((HD, kv_width), jnp.float32),
            pltpu.VMEM((n_ctx, block + STAT_ROWS, HD), jnp.bfloat16),
            pltpu.VMEM((n_ctx, block + STAT_ROWS, HD), jnp.bfloat16),
            pltpu.VMEM((block, HD), jnp.bfloat16),
            pltpu.VMEM((n_ctx, block, HD), jnp.bfloat16),
            pltpu.VMEM((n_head, tokens, columns // n_head), jnp.float32),
            pltpu.VMEM((n_head, tokens, columns // n_head), jnp.float32),
            dma((5,)),
            dma((batch,)),
            dma((batch,)),
            dma((n_ctx,)),
            dma((batch,)),
            dma((batch,)),
            dma((n_ctx,)),
            dma((n_ctx,)),
            dma((n_ctx,)),
            dma((n_ctx,)),
            dma((n_head,)),
            dma((n_head,)),
        ],
        compiler_params=pltpu.CompilerParams(
            collective_id=0, has_side_effects=True, vmem_limit_bytes=VMEM_BYTES
        ),
        cost_estimate=pl.CostEstimate(
            flops=2 * tokens * features * (columns + 2 * rows),
            bytes_accessed=2 * (2 * k_cache.size + 2 * v_cache.size + out_weight.size),
            transcendentals=tokens * heads * rows,
        ),
    )(*[
        pltpu.with_memory_space_constraint(x, pltpu.HBM)
        for x in (
            fill.reshape(batch), owner, queries, k_cache, v_cache, new_keys, new_values, out_weight
        )
    ])
    return pl.pallas_call(
        write_kernel,
        out_shape=shapes,
        in_specs=[whole] * 3,
        out_specs=(whole,) * 3,
        scratch_shapes=[dma((2 * batch + 1,))],
        compiler_params=pltpu.CompilerParams(vmem_limit_bytes=1024 * 1024),
    )(*[pltpu.with_memory_space_constraint(x, pltpu.VMEM) for x in results])


def solution(mesh):
    in_specs = (
        P(None, None, "head"),
        P(None, "ctx", "head"),
        P(None, "ctx", "head"),
        P(None, None, "head"),
        P(None, None, "head"),
        P(None, "ctx"),
        P(),
        P("head", "ctx"),
    )
    out_specs = (P(None, "ctx", "head"), P(None, "ctx", "head"), P(None, None, ("ctx", "head")))
    return jax.shard_map(
        functools.partial(on_device_fused, mesh.shape["ctx"], mesh.shape["head"]), mesh=mesh, in_specs=in_specs, out_specs=out_specs, check_vma=False
    )
```

```python
import functools

import jax
import jax.numpy as jnp
from jax import lax
from jax.experimental import pallas as pl
from jax.experimental.pallas import tpu as pltpu
from jax.sharding import PartitionSpec as P

HD = 128


def on_device(queries, k_cache, v_cache, new_keys, new_values, fill, owner, out_weight):
    steps, batch = owner.shape
    rows = k_cache.shape[1]
    device_pos = lax.axis_index("ctx")
    mine = (owner == device_pos).astype(jnp.int32)
    seen = jnp.cumsum(mine, axis=0)
    local_fill = fill[:, 0]
    slot = local_fill[None, :] + seen - 1
    row_ids = lax.broadcasted_iota(jnp.int32, (batch, rows), 1)
    keys_out, values_out = (k_cache, v_cache)
    for step in range(steps):
        target = ((row_ids == slot[step][:, None]) & (mine[step][:, None] == 1))[:, :, None]
        keys_out = jnp.where(target, new_keys[step][:, None, :], keys_out)
        values_out = jnp.where(target, new_values[step][:, None, :], values_out)
    lengths = local_fill[None, :] + seen
    kv_local = keys_out.shape[2] // HD
    groups = queries.shape[2] // (kv_local * HD)
    query_heads = queries.reshape(steps, batch, kv_local, groups, HD)
    key_heads = keys_out.reshape(batch, rows, kv_local, HD)
    value_heads = values_out.reshape(batch, rows, kv_local, HD)
    scores = jnp.einsum(
        "sbgqd,brgd->sbgqr", query_heads, key_heads, preferred_element_type=jnp.float32
    ) * (1.0 / HD**0.5)
    slot_ids = lax.broadcasted_iota(jnp.int32, (1, 1, 1, 1, rows), 4)
    live = slot_ids < lengths[:, :, None, None, None]
    masked = jnp.where(live, scores, -1e30)
    peak = jnp.max(masked, axis=-1)
    weights = jnp.where(live, jnp.exp(masked - peak[..., None]), 0.0)
    total = jnp.sum(weights, axis=-1)
    rounded = weights.astype(jnp.bfloat16)
    numer = jnp.einsum(
        "sbgqr,brgd->sbgqd", rounded, value_heads, preferred_element_type=jnp.float32
    )
    largest = lax.pmax(peak, "ctx")
    factor = jnp.exp(peak - largest)
    numer_all, total_all = lax.psum((numer * factor[..., None], total * factor), "ctx")
    attention = (numer_all / total_all[..., None]).astype(jnp.bfloat16)
    attention_rows = attention.reshape(steps * batch, kv_local * groups * HD)
    partial_out = jnp.dot(attention_rows, out_weight, preferred_element_type=jnp.float32)
    mixed = lax.psum_scatter(partial_out, "head", scatter_dimension=1, tiled=True).astype(
        jnp.bfloat16
    )
    return (keys_out, values_out, mixed.reshape(steps, batch, -1))


MESH = pl.DeviceIdType.MESH
STAT_ROWS = 16
VMEM_BYTES = 32 * 1024 * 1024


def new_rows(old, slots, rows_f32, step_rows):
    ids = lax.broadcasted_iota(jnp.int32, old.shape, 0).astype(jnp.int16)
    for slot, row in zip(slots, step_rows):
        new = jnp.broadcast_to(rows_f32[row : row + 1, :], (16, old.shape[1])).astype(old.dtype)
        new = jnp.concatenate([new] * (old.shape[0] // 16), axis=0)
        old = jnp.where(ids == jnp.full(old.shape, slot, jnp.int32).astype(jnp.int16), new, old)
    return old


def fused_kernel(
    n_ctx, n_head, steps, batch, groups, kv_local,
    fill_hbm, owner_hbm, q_hbm, k_hbm, v_hbm, nk_hbm, nv_hbm, w_hbm,
    k_out, v_out, mixed,
    fill, owner, q_v, nk_v, nv_v, k_v, v_v, w_v, q_rows, part, stat, nk_f, nv_f,
    send1, recv1, send2, recv2, send3, recv3,
    small_sem, k_sem, v_sem, w_sem,
    ssem1, rsem1, ssem2, rsem2, ssem3, rsem3,
):
    me = lax.axis_index("ctx")
    hme = lax.axis_index("head")
    tokens = steps * batch
    rows = k_v.shape[1]
    heads = groups * kv_local
    per = heads // n_ctx
    block = per * tokens
    depth = per * HD
    width = mixed.shape[2]

    smalls = [
        pltpu.make_async_copy(q_hbm, q_v, small_sem.at[0]),
        pltpu.make_async_copy(nk_hbm, nk_v, small_sem.at[1]),
        pltpu.make_async_copy(nv_hbm, nv_v, small_sem.at[2]),
        pltpu.make_async_copy(fill_hbm, fill, small_sem.at[3]),
        pltpu.make_async_copy(owner_hbm, owner, small_sem.at[4]),
    ]
    k_in = [pltpu.make_async_copy(k_hbm.at[b], k_v.at[b], k_sem.at[b]) for b in range(batch)]
    v_in = [pltpu.make_async_copy(v_hbm.at[b], v_v.at[b], v_sem.at[b]) for b in range(batch)]
    w_in = [
        pltpu.make_async_copy(w_hbm.at[pl.ds(c * depth, depth), :], w_v.at[c], w_sem.at[c])
        for c in range(n_ctx)
    ]
    smalls[0].start()
    for copy in k_in:
        copy.start()
    for copy in smalls[1:]:
        copy.start()
    for copy in v_in:
        copy.start()
    for copy in w_in:
        copy.start()

    barrier = pltpu.get_barrier_semaphore()
    for d in range(1, n_ctx):
        pl.semaphore_signal(barrier, inc=1, device_id={"ctx": lax.rem(me + d, n_ctx)}, device_id_type=MESH)
    for d in range(1, n_head):
        pl.semaphore_signal(barrier, inc=1, device_id={"head": lax.rem(hme + d, n_head)}, device_id_type=MESH)

    smalls[0].wait()
    for s in range(steps):
        q_f = q_v[s].astype(jnp.float32)
        for h in range(heads):
            q_rows[h * tokens + s * batch : h * tokens + (s + 1) * batch, :] = q_f[:, h * HD : (h + 1) * HD]
    smalls[1].wait()
    smalls[2].wait()
    nk_f[...] = jnp.zeros_like(nk_f)
    nv_f[...] = jnp.zeros_like(nv_f)
    for s in range(steps):
        nk_f[s * batch : (s + 1) * batch, :] = nk_v[s].astype(jnp.float32)
        nv_f[s * batch : (s + 1) * batch, :] = nv_v[s].astype(jnp.float32)

    live_rows = groups * steps
    slot_ids = lax.broadcasted_iota(jnp.int32, (live_rows, rows), 1)
    lane = lax.broadcasted_iota(jnp.int32, (live_rows, HD), 1)
    even = lax.rem(lane, 2) == 0
    step_ids = lax.rem(lax.broadcasted_iota(jnp.int32, (live_rows, HD), 0), steps)
    pick = (
        lax.broadcasted_iota(jnp.int32, (STAT_ROWS, HD), 0)
        == lax.broadcasted_iota(jnp.int32, (STAT_ROWS, HD), 1)
    ).astype(jnp.bfloat16)

    smalls[3].wait()
    smalls[4].wait()
    slots = []
    mine_ids = jnp.full((live_rows, HD), steps, jnp.int32)
    for b in range(batch):
        seen = fill[b]
        slots_b = []
        for s in range(steps):
            mine = owner[s, b] == me
            slots_b.append(jnp.where(mine, seen, -1))
            seen = seen + jnp.where(mine, 1, 0)
            mine_ids = jnp.where(lane == s * batch + b, jnp.where(mine, s, steps), mine_ids)
        slots.append(slots_b)
    visible = mine_ids <= step_ids
    new_live = [visible & (lax.rem(lane, batch) == b) for b in range(batch)]

    def first(c):
        d = lax.rem(c - me + n_ctx, n_ctx)
        return pltpu.make_async_remote_copy(
            src_ref=send1.at[c], dst_ref=recv1.at[d], send_sem=ssem1.at[c], recv_sem=rsem1.at[d],
            device_id={"ctx": c}, device_id_type=MESH,
        )

    all_b = range(batch)
    sent = 0
    for g in range(kv_local):
        cols = slice(g * HD, (g + 1) * HD)
        nk_g = nk_f[:, cols].astype(jnp.bfloat16)
        nv_g = nv_f[:, cols].astype(jnp.bfloat16)
        at = [pl.ds(g * groups * tokens + b, live_rows, stride=batch) for b in all_b]
        query = [q_rows[at[b], :].astype(jnp.bfloat16) for b in all_b]
        if g == 0:
            for copy in k_in:
                copy.wait()
        scores = [
            lax.dot_general(
                query[b], k_v[b, :, cols], (((1,), (1,)), ((), ())),
                preferred_element_type=jnp.float32,
            )
            for b in all_b
        ]
        new_scores = [
            lax.dot_general(
                query[b], nk_g, (((1,), (1,)), ((), ())), preferred_element_type=jnp.float32
            )
            for b in all_b
        ]
        masked = [
            jnp.where(slot_ids < fill[b], scores[b] * (1.0 / HD**0.5), -1e30) for b in all_b
        ]
        new_masked = [
            jnp.where(new_live[b], new_scores[b] * (1.0 / HD**0.5), -1e30) for b in all_b
        ]
        peak = [
            jnp.maximum(
                jnp.max(masked[b], axis=1, keepdims=True),
                jnp.max(new_masked[b], axis=1, keepdims=True),
            )
            for b in all_b
        ]
        weights = [jnp.exp(masked[b] - peak[b]) for b in all_b]
        new_weights = [jnp.exp(new_masked[b] - peak[b]) for b in all_b]
        total = [
            jnp.sum(weights[b], axis=1, keepdims=True)
            + jnp.sum(new_weights[b], axis=1, keepdims=True)
            for b in all_b
        ]
        if g == 0:
            for copy in v_in:
                copy.wait()
        sums = [
            jnp.dot(
                weights[b].astype(jnp.bfloat16), v_v[b, :, cols],
                preferred_element_type=jnp.float32,
            )
            + jnp.dot(
                new_weights[b].astype(jnp.bfloat16), nv_g, preferred_element_type=jnp.float32
            )
            for b in all_b
        ]
        for b in all_b:
            part[at[b], :] = sums[b]
        for b in all_b:
            both = jnp.where(even, peak[b], total[b])
            high = both.astype(jnp.bfloat16).astype(jnp.float32)
            middle = (both - high).astype(jnp.bfloat16).astype(jnp.float32)
            low = both - high - middle
            stat[at[b], :] = jnp.where(lane < 2, high, jnp.where(lane < 4, middle, low))
        ready = n_ctx * (g + 1) // kv_local
        for c in range(sent, ready):
            here = slice(c * block, (c + 1) * block)
            send1[c, 0:block, :] = part[here, :].astype(jnp.bfloat16)
            turned = lax.dot_general(
                pick, stat[here, :].astype(jnp.bfloat16), (((1,), (1,)), ((), ())),
                preferred_element_type=jnp.float32,
            )
            send1[c, block : block + STAT_ROWS, 0:block] = turned.astype(jnp.bfloat16)
        if g == 0:
            pl.semaphore_wait(barrier, n_ctx + n_head - 2)
        for c in range(sent, ready):

            @pl.when(me != c)
            def _(c=c):
                first(c).start()

        sent = ready

    own_rows = [[s * batch + b for s in range(steps)] for b in all_b]
    for b in all_b:
        k_out[b] = new_rows(k_v[b], slots[b], nk_f, own_rows[b])

    recv1[0] = send1[me]
    for d in range(1, n_ctx):
        pltpu.make_async_remote_copy(
            src_ref=send1.at[0], dst_ref=recv1.at[d], send_sem=ssem1.at[0], recv_sem=rsem1.at[d],
            device_id={"ctx": lax.rem(me + d, n_ctx)}, device_id_type=MESH,
        ).wait_recv()
    peaks, totals = [], []
    for d in range(n_ctx):
        got = recv1[d, block : block + STAT_ROWS, 0:block].astype(jnp.float32)
        peaks.append(got[0:1] + got[2:3] + got[4:5])
        totals.append(got[1:2] + got[3:4] + got[5:6])
    peaks = jnp.concatenate(peaks, axis=0)
    totals = jnp.concatenate(totals, axis=0)
    factor = jnp.exp(peaks - jnp.max(peaks, axis=0, keepdims=True))
    shares = factor / jnp.sum(factor * totals, axis=0, keepdims=True)
    shares = jnp.transpose(shares)
    attention = jnp.zeros((block, HD), jnp.float32)
    for d in range(n_ctx):
        attention += recv1[d, 0:block, :].astype(jnp.float32) * shares[:, d : d + 1]
    send2[...] = attention.astype(jnp.bfloat16)

    seconds = {}
    for d in sorted(range(1, n_ctx), key=lambda d: -min(d, n_ctx - d)):
        seconds[d] = pltpu.make_async_remote_copy(
            src_ref=send2, dst_ref=recv2.at[d], send_sem=ssem2.at[d], recv_sem=rsem2.at[d],
            device_id={"ctx": lax.rem(me + d, n_ctx)}, device_id_type=MESH,
        )
        seconds[d].start()
    for b in all_b:
        v_out[b] = new_rows(v_v[b], slots[b], nv_f, own_rows[b])
    for copy in w_in:
        copy.wait()
    order = [0] + sorted(range(1, n_ctx), key=lambda d: min(d, n_ctx - d))
    share = None
    for d in order:
        if d > 0:
            seconds[d].wait_recv()
            got = recv2[d].astype(jnp.float32)
        else:
            got = send2[...].astype(jnp.float32)
        features = jnp.concatenate(
            [got[i * tokens : (i + 1) * tokens] for i in range(per)], axis=1
        ).astype(jnp.bfloat16)
        source = lax.rem(me - d + n_ctx, n_ctx)
        if d == order[-1]:
            break
        product = jnp.dot(features, w_v[source], preferred_element_type=jnp.float32)
        share = product if share is None else share + product
    for h in range(n_head):
        send3[h] = share[:, h * width : (h + 1) * width]
    third = []
    for d in sorted(range(n_head), key=lambda d: -min(d, n_head - d)):
        target = lax.rem(hme + d, n_head)
        columns = pl.ds(pl.multiple_of(target * width, width), width)
        send3[target] = send3[target] + jnp.dot(
            features, w_v[source, :, columns], preferred_element_type=jnp.float32
        )
        if d > 0:
            copy = pltpu.make_async_remote_copy(
                src_ref=send3.at[target], dst_ref=recv3.at[d], send_sem=ssem3.at[d], recv_sem=rsem3.at[d],
                device_id={"head": target}, device_id_type=MESH,
            )
            copy.start()
            third.append(copy)
    result = send3[hme]
    for copy in third:
        copy.wait_recv()
    for d in range(1, n_head):
        result += recv3[d]
    result = result.astype(mixed.dtype)
    for s in range(steps):
        mixed[s] = result[s * batch : (s + 1) * batch]

    for c in range(n_ctx):

        @pl.when(me != c)
        def _(c=c):
            first(c).wait_send()

    for copy in seconds.values():
        copy.wait_send()
    for copy in third:
        copy.wait_send()


def write_kernel(k_in, v_in, m_in, k_out, v_out, m_out, sems):
    batch = k_in.shape[0]
    copies = [pltpu.make_async_copy(m_in, m_out, sems.at[2 * batch])]
    for b in range(batch):
        copies.append(pltpu.make_async_copy(k_in.at[b], k_out.at[b], sems.at[b]))
        copies.append(pltpu.make_async_copy(v_in.at[b], v_out.at[b], sems.at[batch + b]))
    for copy in copies:
        copy.start()
    for copy in copies:
        copy.wait()


def on_device_fused(
    n_ctx, n_head, queries, k_cache, v_cache, new_keys, new_values, fill, owner, out_weight
):
    steps, batch, features = queries.shape
    rows, kv_width = k_cache.shape[1:]
    kv_local = kv_width // HD
    heads = features // HD
    tokens = steps * batch
    columns = out_weight.shape[1]
    per = heads // n_ctx
    block = per * tokens
    if heads % n_ctx or block % 16 or block > HD or n_ctx % kv_local or batch != 8 or tokens > HD or columns % (n_head * HD):
        return on_device(
            queries, k_cache, v_cache, new_keys, new_values, fill, owner, out_weight
        )
    kernel = functools.partial(
        fused_kernel, n_ctx, n_head, steps, batch, heads // kv_local, kv_local
    )
    whole = pl.BlockSpec(memory_space=pl.ANY)
    dma = pltpu.SemaphoreType.DMA
    shapes = (
        jax.ShapeDtypeStruct(k_cache.shape, k_cache.dtype),
        jax.ShapeDtypeStruct(v_cache.shape, v_cache.dtype),
        jax.ShapeDtypeStruct((steps, batch, columns // n_head), jnp.bfloat16),
    )
    results = pl.pallas_call(
        kernel,
        out_shape=shapes,
        in_specs=[whole] * 8,
        out_specs=(pl.BlockSpec(memory_space=pltpu.VMEM),) * 3,
        scratch_shapes=[
            pltpu.SMEM((batch,), jnp.int32),
            pltpu.SMEM((steps, batch), jnp.int32),
            pltpu.VMEM(queries.shape, jnp.bfloat16),
            pltpu.VMEM(new_keys.shape, jnp.bfloat16),
            pltpu.VMEM(new_values.shape, jnp.bfloat16),
            pltpu.VMEM(k_cache.shape, jnp.bfloat16),
            pltpu.VMEM(v_cache.shape, jnp.bfloat16),
            pltpu.VMEM((n_ctx, per * HD, columns), jnp.bfloat16),
            pltpu.VMEM((heads * tokens, HD), jnp.float32),
            pltpu.VMEM((heads * tokens, HD), jnp.float32),
            pltpu.VMEM((heads * tokens, HD), jnp.float32),
            pltpu.VMEM((HD, kv_width), jnp.float32),
            pltpu.VMEM((HD, kv_width), jnp.float32),
            pltpu.VMEM((n_ctx, block + STAT_ROWS, HD), jnp.bfloat16),
            pltpu.VMEM((n_ctx, block + STAT_ROWS, HD), jnp.bfloat16),
            pltpu.VMEM((block, HD), jnp.bfloat16),
            pltpu.VMEM((n_ctx, block, HD), jnp.bfloat16),
            pltpu.VMEM((n_head, tokens, columns // n_head), jnp.float32),
            pltpu.VMEM((n_head, tokens, columns // n_head), jnp.float32),
            dma((5,)),
            dma((batch,)),
            dma((batch,)),
            dma((n_ctx,)),
            dma((n_ctx,)),
            dma((n_ctx,)),
            dma((n_ctx,)),
            dma((n_ctx,)),
            dma((n_head,)),
            dma((n_head,)),
        ],
        compiler_params=pltpu.CompilerParams(
            collective_id=0, has_side_effects=True, vmem_limit_bytes=VMEM_BYTES
        ),
        cost_estimate=pl.CostEstimate(
            flops=2 * tokens * features * (columns + 2 * rows),
            bytes_accessed=2 * (2 * k_cache.size + 2 * v_cache.size + out_weight.size),
            transcendentals=tokens * heads * rows,
        ),
    )(*[
        pltpu.with_memory_space_constraint(x, pltpu.HBM)
        for x in (
            fill.reshape(batch), owner, queries, k_cache, v_cache, new_keys, new_values, out_weight
        )
    ])
    return pl.pallas_call(
        write_kernel,
        out_shape=shapes,
        in_specs=[whole] * 3,
        out_specs=(whole,) * 3,
        scratch_shapes=[dma((2 * batch + 1,))],
        compiler_params=pltpu.CompilerParams(vmem_limit_bytes=1024 * 1024),
    )(*[pltpu.with_memory_space_constraint(x, pltpu.VMEM) for x in results])


def solution(mesh):
    in_specs = (
        P(None, None, "head"),
        P(None, "ctx", "head"),
        P(None, "ctx", "head"),
        P(None, None, "head"),
        P(None, None, "head"),
        P(None, "ctx"),
        P(),
        P("head", "ctx"),
    )
    out_specs = (P(None, "ctx", "head"), P(None, "ctx", "head"), P(None, None, ("ctx", "head")))
    return jax.shard_map(
        functools.partial(on_device_fused, mesh.shape["ctx"], mesh.shape["head"]), mesh=mesh, in_specs=in_specs, out_specs=out_specs, check_vma=False
    )
```

```python
import functools

import jax
import jax.numpy as jnp
from jax import lax
from jax.experimental import pallas as pl
from jax.experimental.pallas import tpu as pltpu
from jax.sharding import PartitionSpec as P

HD = 128


def on_device(queries, k_cache, v_cache, new_keys, new_values, fill, owner, out_weight):
    steps, batch = owner.shape
    rows = k_cache.shape[1]
    device_pos = lax.axis_index("ctx")
    mine = (owner == device_pos).astype(jnp.int32)
    seen = jnp.cumsum(mine, axis=0)
    local_fill = fill[:, 0]
    slot = local_fill[None, :] + seen - 1
    row_ids = lax.broadcasted_iota(jnp.int32, (batch, rows), 1)
    keys_out, values_out = (k_cache, v_cache)
    for step in range(steps):
        target = ((row_ids == slot[step][:, None]) & (mine[step][:, None] == 1))[:, :, None]
        keys_out = jnp.where(target, new_keys[step][:, None, :], keys_out)
        values_out = jnp.where(target, new_values[step][:, None, :], values_out)
    lengths = local_fill[None, :] + seen
    kv_local = keys_out.shape[2] // HD
    groups = queries.shape[2] // (kv_local * HD)
    query_heads = queries.reshape(steps, batch, kv_local, groups, HD)
    key_heads = keys_out.reshape(batch, rows, kv_local, HD)
    value_heads = values_out.reshape(batch, rows, kv_local, HD)
    scores = jnp.einsum(
        "sbgqd,brgd->sbgqr", query_heads, key_heads, preferred_element_type=jnp.float32
    ) * (1.0 / HD**0.5)
    slot_ids = lax.broadcasted_iota(jnp.int32, (1, 1, 1, 1, rows), 4)
    live = slot_ids < lengths[:, :, None, None, None]
    masked = jnp.where(live, scores, -1e30)
    peak = jnp.max(masked, axis=-1)
    weights = jnp.where(live, jnp.exp(masked - peak[..., None]), 0.0)
    total = jnp.sum(weights, axis=-1)
    rounded = weights.astype(jnp.bfloat16)
    numer = jnp.einsum(
        "sbgqr,brgd->sbgqd", rounded, value_heads, preferred_element_type=jnp.float32
    )
    largest = lax.pmax(peak, "ctx")
    factor = jnp.exp(peak - largest)
    numer_all, total_all = lax.psum((numer * factor[..., None], total * factor), "ctx")
    attention = (numer_all / total_all[..., None]).astype(jnp.bfloat16)
    attention_rows = attention.reshape(steps * batch, kv_local * groups * HD)
    partial_out = jnp.dot(attention_rows, out_weight, preferred_element_type=jnp.float32)
    mixed = lax.psum_scatter(partial_out, "head", scatter_dimension=1, tiled=True).astype(
        jnp.bfloat16
    )
    return (keys_out, values_out, mixed.reshape(steps, batch, -1))


MESH = pl.DeviceIdType.MESH
STAT_ROWS = 16
VMEM_BYTES = 32 * 1024 * 1024


def new_rows(old, slots, rows_f32, step_rows):
    ids = lax.broadcasted_iota(jnp.int32, old.shape, 0).astype(jnp.int16)
    for slot, row in zip(slots, step_rows):
        new = jnp.broadcast_to(rows_f32[row : row + 1, :], (16, old.shape[1])).astype(old.dtype)
        new = jnp.concatenate([new] * (old.shape[0] // 16), axis=0)
        old = jnp.where(ids == jnp.full(old.shape, slot, jnp.int32).astype(jnp.int16), new, old)
    return old


def partner(index, e, size):
    total, bit = 0, 1
    while bit < size:
        here = lax.rem(lax.div(index, bit), 2)
        total = total + bit * (1 - here if e // bit % 2 else here)
        bit *= 2
    return total


def fused_kernel(
    n_ctx, n_head, steps, batch, groups, kv_local,
    fill_hbm, owner_hbm, q_hbm, k_hbm, v_hbm, nk_hbm, nv_hbm, w_hbm,
    k_out, v_out, mixed,
    fill, owner, q_v, nk_v, nv_v, k_v, v_v, w_v, q_rows, part, stat, nk_f, nv_f,
    send1, recv1, send2, recv2, send3, recv3,
    small_sem, k_sem, v_sem, w_sem,
    ssem1, rsem1, ssem2, rsem2, ssem3, rsem3,
):
    me = lax.axis_index("ctx")
    hme = lax.axis_index("head")
    tokens = steps * batch
    rows = k_v.shape[1]
    heads = groups * kv_local
    per = heads // n_ctx
    block = per * tokens
    depth = per * HD
    width = mixed.shape[2]

    smalls = [
        pltpu.make_async_copy(q_hbm, q_v, small_sem.at[0]),
        pltpu.make_async_copy(nk_hbm, nk_v, small_sem.at[1]),
        pltpu.make_async_copy(nv_hbm, nv_v, small_sem.at[2]),
        pltpu.make_async_copy(fill_hbm, fill, small_sem.at[3]),
        pltpu.make_async_copy(owner_hbm, owner, small_sem.at[4]),
    ]
    k_in = [pltpu.make_async_copy(k_hbm.at[b], k_v.at[b], k_sem.at[b]) for b in range(batch)]
    v_in = [pltpu.make_async_copy(v_hbm.at[b], v_v.at[b], v_sem.at[b]) for b in range(batch)]
    w_in = [
        pltpu.make_async_copy(w_hbm.at[pl.ds(c * depth, depth), :], w_v.at[c], w_sem.at[c])
        for c in range(n_ctx)
    ]
    smalls[0].start()
    for copy in k_in:
        copy.start()
    for copy in smalls[1:]:
        copy.start()
    for copy in v_in:
        copy.start()
    for copy in w_in:
        copy.start()

    barrier = pltpu.get_barrier_semaphore()
    for d in range(1, n_ctx):
        pl.semaphore_signal(barrier, inc=1, device_id={"ctx": lax.rem(me + d, n_ctx)}, device_id_type=MESH)
    for d in range(1, n_head):
        pl.semaphore_signal(barrier, inc=1, device_id={"head": lax.rem(hme + d, n_head)}, device_id_type=MESH)

    smalls[0].wait()
    for s in range(steps):
        q_f = q_v[s].astype(jnp.float32)
        for h in range(heads):
            q_rows[h * tokens + s * batch : h * tokens + (s + 1) * batch, :] = q_f[:, h * HD : (h + 1) * HD]
    smalls[1].wait()
    smalls[2].wait()
    nk_f[...] = jnp.zeros_like(nk_f)
    nv_f[...] = jnp.zeros_like(nv_f)
    for s in range(steps):
        nk_f[s * batch : (s + 1) * batch, :] = nk_v[s].astype(jnp.float32)
        nv_f[s * batch : (s + 1) * batch, :] = nv_v[s].astype(jnp.float32)

    live_rows = groups * steps
    slot_ids = lax.broadcasted_iota(jnp.int32, (live_rows, rows), 1)
    lane = lax.broadcasted_iota(jnp.int32, (live_rows, HD), 1)
    even = lax.rem(lane, 2) == 0
    step_ids = lax.rem(lax.broadcasted_iota(jnp.int32, (live_rows, HD), 0), steps)
    pick = (
        lax.broadcasted_iota(jnp.int32, (STAT_ROWS, HD), 0)
        == lax.broadcasted_iota(jnp.int32, (STAT_ROWS, HD), 1)
    ).astype(jnp.bfloat16)

    smalls[3].wait()
    smalls[4].wait()
    slots = []
    mine_ids = jnp.full((live_rows, HD), steps, jnp.int32)
    for b in range(batch):
        seen = fill[b]
        slots_b = []
        for s in range(steps):
            mine = owner[s, b] == me
            slots_b.append(jnp.where(mine, seen, -1))
            seen = seen + jnp.where(mine, 1, 0)
            mine_ids = jnp.where(lane == s * batch + b, jnp.where(mine, s, steps), mine_ids)
        slots.append(slots_b)
    visible = mine_ids <= step_ids
    new_live = [visible & (lax.rem(lane, batch) == b) for b in range(batch)]

    peers = [partner(me, e, n_ctx) for e in range(n_ctx)]
    firsts = [None] + [
        pltpu.make_async_remote_copy(
            src_ref=send1.at[e], dst_ref=recv1.at[e], send_sem=ssem1.at[e], recv_sem=rsem1.at[e],
            device_id={"ctx": peers[e]}, device_id_type=MESH,
        )
        for e in range(1, n_ctx)
    ]
    all_b = range(batch)
    far_first = list(range(kv_local))[::-1]
    per_group = n_ctx // kv_local
    for turn in far_first:
        g = partner(lax.div(me, per_group), turn, kv_local)
        cols = pl.ds(pl.multiple_of(g * HD, HD), HD)
        nk_g = nk_f[:, cols].astype(jnp.bfloat16)
        nv_g = nv_f[:, cols].astype(jnp.bfloat16)
        at = [pl.ds(g * groups * tokens + b, live_rows, stride=batch) for b in all_b]
        query = [q_rows[at[b], :].astype(jnp.bfloat16) for b in all_b]
        if turn == far_first[0]:
            for copy in k_in:
                copy.wait()
        scores = [
            lax.dot_general(
                query[b], k_v[b, :, cols], (((1,), (1,)), ((), ())),
                preferred_element_type=jnp.float32,
            )
            for b in all_b
        ]
        new_scores = [
            lax.dot_general(
                query[b], nk_g, (((1,), (1,)), ((), ())), preferred_element_type=jnp.float32
            )
            for b in all_b
        ]
        masked = [
            jnp.where(slot_ids < fill[b], scores[b] * (1.0 / HD**0.5), -1e30) for b in all_b
        ]
        new_masked = [
            jnp.where(new_live[b], new_scores[b] * (1.0 / HD**0.5), -1e30) for b in all_b
        ]
        peak = [
            jnp.maximum(
                jnp.max(masked[b], axis=1, keepdims=True),
                jnp.max(new_masked[b], axis=1, keepdims=True),
            )
            for b in all_b
        ]
        weights = [jnp.exp(masked[b] - peak[b]) for b in all_b]
        new_weights = [jnp.exp(new_masked[b] - peak[b]) for b in all_b]
        total = [
            jnp.sum(weights[b], axis=1, keepdims=True)
            + jnp.sum(new_weights[b], axis=1, keepdims=True)
            for b in all_b
        ]
        if turn == far_first[0]:
            for copy in v_in:
                copy.wait()
        sums = [
            jnp.dot(
                weights[b].astype(jnp.bfloat16), v_v[b, :, cols],
                preferred_element_type=jnp.float32,
            )
            + jnp.dot(
                new_weights[b].astype(jnp.bfloat16), nv_g, preferred_element_type=jnp.float32
            )
            for b in all_b
        ]
        for b in all_b:
            part[at[b], :] = sums[b]
        for b in all_b:
            both = jnp.where(even, peak[b], total[b])
            high = both.astype(jnp.bfloat16).astype(jnp.float32)
            middle = (both - high).astype(jnp.bfloat16).astype(jnp.float32)
            low = both - high - middle
            stat[at[b], :] = jnp.where(lane < 2, high, jnp.where(lane < 4, middle, low))
        group = range((turn + 1) * per_group - 1, turn * per_group - 1, -1)
        for e in group:
            here = pl.ds(pl.multiple_of(peers[e] * block, 8), block)
            to = send1 if e else recv1
            to[e, 0:block, :] = part[here, :].astype(jnp.bfloat16)
            turned = lax.dot_general(
                pick, stat[here, :].astype(jnp.bfloat16), (((1,), (1,)), ((), ())),
                preferred_element_type=jnp.float32,
            )
            to[e, block : block + STAT_ROWS, 0:block] = turned.astype(jnp.bfloat16)
        if turn == far_first[0]:
            pl.semaphore_wait(barrier, n_ctx + n_head - 2)
        for e in group:
            if e:
                firsts[e].start()

    own_rows = [[s * batch + b for s in range(steps)] for b in all_b]
    for b in all_b:
        k_out[b] = new_rows(k_v[b], slots[b], nk_f, own_rows[b])

    for e in range(1, n_ctx):
        firsts[e].wait_recv()
    peaks, totals = [], []
    for d in range(n_ctx):
        got = recv1[d, block : block + STAT_ROWS, 0:block].astype(jnp.float32)
        peaks.append(got[0:1] + got[2:3] + got[4:5])
        totals.append(got[1:2] + got[3:4] + got[5:6])
    peaks = jnp.concatenate(peaks, axis=0)
    totals = jnp.concatenate(totals, axis=0)
    factor = jnp.exp(peaks - jnp.max(peaks, axis=0, keepdims=True))
    shares = factor / jnp.sum(factor * totals, axis=0, keepdims=True)
    shares = jnp.transpose(shares)
    attention = jnp.zeros((block, HD), jnp.float32)
    for d in range(n_ctx):
        attention += recv1[d, 0:block, :].astype(jnp.float32) * shares[:, d : d + 1]
    send2[...] = attention.astype(jnp.bfloat16)

    seconds = {}
    for d in range(n_ctx - 1, 0, -1):
        seconds[d] = pltpu.make_async_remote_copy(
            src_ref=send2, dst_ref=recv2.at[d], send_sem=ssem2.at[d], recv_sem=rsem2.at[d],
            device_id={"ctx": peers[d]}, device_id_type=MESH,
        )
        seconds[d].start()
    for b in all_b:
        v_out[b] = new_rows(v_v[b], slots[b], nv_f, own_rows[b])
    for copy in w_in:
        copy.wait()
    order = list(range(n_ctx))
    share = None
    for d in order:
        if d > 0:
            seconds[d].wait_recv()
            got = recv2[d].astype(jnp.float32)
        else:
            got = send2[...].astype(jnp.float32)
        features = jnp.concatenate(
            [got[i * tokens : (i + 1) * tokens] for i in range(per)], axis=1
        ).astype(jnp.bfloat16)
        source = peers[d]
        if d == order[-1]:
            break
        product = jnp.dot(features, w_v[source], preferred_element_type=jnp.float32)
        share = product if share is None else share + product
    for h in range(n_head):
        send3[h] = share[:, h * width : (h + 1) * width]
    third = []
    for d in sorted(range(n_head), key=lambda d: -min(d, n_head - d)):
        target = lax.rem(hme + d, n_head)
        columns = pl.ds(pl.multiple_of(target * width, width), width)
        send3[target] = send3[target] + jnp.dot(
            features, w_v[source, :, columns], preferred_element_type=jnp.float32
        )
        if d > 0:
            copy = pltpu.make_async_remote_copy(
                src_ref=send3.at[target], dst_ref=recv3.at[d], send_sem=ssem3.at[d], recv_sem=rsem3.at[d],
                device_id={"head": target}, device_id_type=MESH,
            )
            copy.start()
            third.append(copy)
    result = send3[hme]
    for copy in third:
        copy.wait_recv()
    for d in range(1, n_head):
        result += recv3[d]
    result = result.astype(mixed.dtype)
    for s in range(steps):
        mixed[s] = result[s * batch : (s + 1) * batch]

    for copy in firsts[1:]:
        copy.wait_send()
    for copy in seconds.values():
        copy.wait_send()
    for copy in third:
        copy.wait_send()


def write_kernel(k_in, v_in, m_in, k_out, v_out, m_out, sems):
    batch = k_in.shape[0]
    copies = [pltpu.make_async_copy(m_in, m_out, sems.at[2 * batch])]
    for b in range(batch):
        copies.append(pltpu.make_async_copy(k_in.at[b], k_out.at[b], sems.at[b]))
        copies.append(pltpu.make_async_copy(v_in.at[b], v_out.at[b], sems.at[batch + b]))
    for copy in copies:
        copy.start()
    for copy in copies:
        copy.wait()


def on_device_fused(
    n_ctx, n_head, queries, k_cache, v_cache, new_keys, new_values, fill, owner, out_weight
):
    steps, batch, features = queries.shape
    rows, kv_width = k_cache.shape[1:]
    kv_local = kv_width // HD
    heads = features // HD
    tokens = steps * batch
    columns = out_weight.shape[1]
    per = heads // n_ctx
    block = per * tokens
    if heads % n_ctx or block % 16 or block > HD or n_ctx % kv_local or batch != 8 or n_ctx & (n_ctx - 1) or kv_local & (kv_local - 1) or tokens > HD or columns % (n_head * HD):
        return on_device(
            queries, k_cache, v_cache, new_keys, new_values, fill, owner, out_weight
        )
    kernel = functools.partial(
        fused_kernel, n_ctx, n_head, steps, batch, heads // kv_local, kv_local
    )
    whole = pl.BlockSpec(memory_space=pl.ANY)
    dma = pltpu.SemaphoreType.DMA
    shapes = (
        jax.ShapeDtypeStruct(k_cache.shape, k_cache.dtype),
        jax.ShapeDtypeStruct(v_cache.shape, v_cache.dtype),
        jax.ShapeDtypeStruct((steps, batch, columns // n_head), jnp.bfloat16),
    )
    results = pl.pallas_call(
        kernel,
        out_shape=shapes,
        in_specs=[whole] * 8,
        out_specs=(pl.BlockSpec(memory_space=pltpu.VMEM),) * 3,
        scratch_shapes=[
            pltpu.SMEM((batch,), jnp.int32),
            pltpu.SMEM((steps, batch), jnp.int32),
            pltpu.VMEM(queries.shape, jnp.bfloat16),
            pltpu.VMEM(new_keys.shape, jnp.bfloat16),
            pltpu.VMEM(new_values.shape, jnp.bfloat16),
            pltpu.VMEM(k_cache.shape, jnp.bfloat16),
            pltpu.VMEM(v_cache.shape, jnp.bfloat16),
            pltpu.VMEM((n_ctx, per * HD, columns), jnp.bfloat16),
            pltpu.VMEM((heads * tokens, HD), jnp.float32),
            pltpu.VMEM((heads * tokens, HD), jnp.float32),
            pltpu.VMEM((heads * tokens, HD), jnp.float32),
            pltpu.VMEM((HD, kv_width), jnp.float32),
            pltpu.VMEM((HD, kv_width), jnp.float32),
            pltpu.VMEM((n_ctx, block + STAT_ROWS, HD), jnp.bfloat16),
            pltpu.VMEM((n_ctx, block + STAT_ROWS, HD), jnp.bfloat16),
            pltpu.VMEM((block, HD), jnp.bfloat16),
            pltpu.VMEM((n_ctx, block, HD), jnp.bfloat16),
            pltpu.VMEM((n_head, tokens, columns // n_head), jnp.float32),
            pltpu.VMEM((n_head, tokens, columns // n_head), jnp.float32),
            dma((5,)),
            dma((batch,)),
            dma((batch,)),
            dma((n_ctx,)),
            dma((n_ctx,)),
            dma((n_ctx,)),
            dma((n_ctx,)),
            dma((n_ctx,)),
            dma((n_head,)),
            dma((n_head,)),
        ],
        compiler_params=pltpu.CompilerParams(
            collective_id=0, has_side_effects=True, vmem_limit_bytes=VMEM_BYTES
        ),
        cost_estimate=pl.CostEstimate(
            flops=2 * tokens * features * (columns + 2 * rows),
            bytes_accessed=2 * (2 * k_cache.size + 2 * v_cache.size + out_weight.size),
            transcendentals=tokens * heads * rows,
        ),
    )(*[
        pltpu.with_memory_space_constraint(x, pltpu.HBM)
        for x in (
            fill.reshape(batch), owner, queries, k_cache, v_cache, new_keys, new_values, out_weight
        )
    ])
    return pl.pallas_call(
        write_kernel,
        out_shape=shapes,
        in_specs=[whole] * 3,
        out_specs=(whole,) * 3,
        scratch_shapes=[dma((2 * batch + 1,))],
        compiler_params=pltpu.CompilerParams(vmem_limit_bytes=1024 * 1024),
    )(*[pltpu.with_memory_space_constraint(x, pltpu.VMEM) for x in results])


def solution(mesh):
    in_specs = (
        P(None, None, "head"),
        P(None, "ctx", "head"),
        P(None, "ctx", "head"),
        P(None, None, "head"),
        P(None, None, "head"),
        P(None, "ctx"),
        P(),
        P("head", "ctx"),
    )
    out_specs = (P(None, "ctx", "head"), P(None, "ctx", "head"), P(None, None, ("ctx", "head")))
    return jax.shard_map(
        functools.partial(on_device_fused, mesh.shape["ctx"], mesh.shape["head"]), mesh=mesh, in_specs=in_specs, out_specs=out_specs, check_vma=False
    )
```

```python
import functools

import jax
import jax.numpy as jnp
from jax import lax
from jax.experimental import pallas as pl
from jax.experimental.pallas import tpu as pltpu
from jax.sharding import PartitionSpec as P

HD = 128


def on_device(queries, k_cache, v_cache, new_keys, new_values, fill, owner, out_weight):
    steps, batch = owner.shape
    rows = k_cache.shape[1]
    device_pos = lax.axis_index("ctx")
    mine = (owner == device_pos).astype(jnp.int32)
    seen = jnp.cumsum(mine, axis=0)
    local_fill = fill[:, 0]
    slot = local_fill[None, :] + seen - 1
    row_ids = lax.broadcasted_iota(jnp.int32, (batch, rows), 1)
    keys_out, values_out = (k_cache, v_cache)
    for step in range(steps):
        target = ((row_ids == slot[step][:, None]) & (mine[step][:, None] == 1))[:, :, None]
        keys_out = jnp.where(target, new_keys[step][:, None, :], keys_out)
        values_out = jnp.where(target, new_values[step][:, None, :], values_out)
    lengths = local_fill[None, :] + seen
    kv_local = keys_out.shape[2] // HD
    groups = queries.shape[2] // (kv_local * HD)
    query_heads = queries.reshape(steps, batch, kv_local, groups, HD)
    key_heads = keys_out.reshape(batch, rows, kv_local, HD)
    value_heads = values_out.reshape(batch, rows, kv_local, HD)
    scores = jnp.einsum(
        "sbgqd,brgd->sbgqr", query_heads, key_heads, preferred_element_type=jnp.float32
    ) * (1.0 / HD**0.5)
    slot_ids = lax.broadcasted_iota(jnp.int32, (1, 1, 1, 1, rows), 4)
    live = slot_ids < lengths[:, :, None, None, None]
    masked = jnp.where(live, scores, -1e30)
    peak = jnp.max(masked, axis=-1)
    weights = jnp.where(live, jnp.exp(masked - peak[..., None]), 0.0)
    total = jnp.sum(weights, axis=-1)
    rounded = weights.astype(jnp.bfloat16)
    numer = jnp.einsum(
        "sbgqr,brgd->sbgqd", rounded, value_heads, preferred_element_type=jnp.float32
    )
    largest = lax.pmax(peak, "ctx")
    factor = jnp.exp(peak - largest)
    numer_all, total_all = lax.psum((numer * factor[..., None], total * factor), "ctx")
    attention = (numer_all / total_all[..., None]).astype(jnp.bfloat16)
    attention_rows = attention.reshape(steps * batch, kv_local * groups * HD)
    partial_out = jnp.dot(attention_rows, out_weight, preferred_element_type=jnp.float32)
    mixed = lax.psum_scatter(partial_out, "head", scatter_dimension=1, tiled=True).astype(
        jnp.bfloat16
    )
    return (keys_out, values_out, mixed.reshape(steps, batch, -1))


MESH = pl.DeviceIdType.MESH
STAT_ROWS = 16
VMEM_BYTES = 32 * 1024 * 1024


def new_rows(old, slots, rows_f32, step_rows):
    ids = lax.broadcasted_iota(jnp.int32, old.shape, 0).astype(jnp.int16)
    for slot, row in zip(slots, step_rows):
        new = jnp.broadcast_to(rows_f32[row : row + 1, :], (16, old.shape[1])).astype(old.dtype)
        new = jnp.concatenate([new] * (old.shape[0] // 16), axis=0)
        old = jnp.where(ids == jnp.full(old.shape, slot, jnp.int32).astype(jnp.int16), new, old)
    return old


def partner(index, e, size):
    total, bit = 0, 1
    while bit < size:
        here = lax.rem(lax.div(index, bit), 2)
        total = total + bit * (1 - here if e // bit % 2 else here)
        bit *= 2
    return total


def fused_kernel(
    n_ctx, n_head, steps, batch, groups, kv_local,
    fill_hbm, owner_hbm, q_hbm, k_hbm, v_hbm, nk_hbm, nv_hbm, w_hbm,
    k_out, v_out, mixed,
    fill, owner, q_v, nk_v, nv_v, k_v, v_v, w_v, q_rows, part, stat, nk_f, nv_f,
    send1, recv1, send2, recv2, send3, recv3, send4, recv4,
    small_sem, k_sem, v_sem, w_sem,
    ssem1, rsem1, ssem2, rsem2, ssem3, rsem3,
):
    me = lax.axis_index("ctx")
    hme = lax.axis_index("head")
    tokens = steps * batch
    rows = k_v.shape[1]
    heads = groups * kv_local
    per = heads // n_ctx
    block = per * tokens
    depth = per * HD
    width = mixed.shape[2]

    smalls = [
        pltpu.make_async_copy(q_hbm, q_v, small_sem.at[0]),
        pltpu.make_async_copy(nk_hbm, nk_v, small_sem.at[1]),
        pltpu.make_async_copy(nv_hbm, nv_v, small_sem.at[2]),
        pltpu.make_async_copy(fill_hbm, fill, small_sem.at[3]),
        pltpu.make_async_copy(owner_hbm, owner, small_sem.at[4]),
    ]
    k_in = [pltpu.make_async_copy(k_hbm.at[b], k_v.at[b], k_sem.at[b]) for b in range(batch)]
    v_in = [pltpu.make_async_copy(v_hbm.at[b], v_v.at[b], v_sem.at[b]) for b in range(batch)]
    w_in = [
        pltpu.make_async_copy(w_hbm.at[pl.ds(c * depth, depth), :], w_v.at[c], w_sem.at[c])
        for c in range(n_ctx)
    ]
    smalls[0].start()
    for copy in k_in:
        copy.start()
    for copy in smalls[1:]:
        copy.start()
    for copy in v_in:
        copy.start()
    for copy in w_in:
        copy.start()

    barrier = pltpu.get_barrier_semaphore()
    for d in range(1, n_ctx):
        pl.semaphore_signal(barrier, inc=1, device_id={"ctx": lax.rem(me + d, n_ctx)}, device_id_type=MESH)
    for d in range(1, n_head):
        pl.semaphore_signal(barrier, inc=1, device_id={"head": lax.rem(hme + d, n_head)}, device_id_type=MESH)

    smalls[0].wait()
    for s in range(steps):
        q_f = q_v[s].astype(jnp.float32)
        for h in range(heads):
            q_rows[h * tokens + s * batch : h * tokens + (s + 1) * batch, :] = q_f[:, h * HD : (h + 1) * HD]
    smalls[1].wait()
    smalls[2].wait()
    nk_f[...] = jnp.zeros_like(nk_f)
    nv_f[...] = jnp.zeros_like(nv_f)
    for s in range(steps):
        nk_f[s * batch : (s + 1) * batch, :] = nk_v[s].astype(jnp.float32)
        nv_f[s * batch : (s + 1) * batch, :] = nv_v[s].astype(jnp.float32)

    live_rows = groups * steps
    slot_ids = lax.broadcasted_iota(jnp.int32, (live_rows, rows), 1)
    lane = lax.broadcasted_iota(jnp.int32, (live_rows, HD), 1)
    even = lax.rem(lane, 2) == 0
    step_ids = lax.rem(lax.broadcasted_iota(jnp.int32, (live_rows, HD), 0), steps)
    pick = (
        lax.broadcasted_iota(jnp.int32, (STAT_ROWS, HD), 0)
        == lax.broadcasted_iota(jnp.int32, (STAT_ROWS, HD), 1)
    ).astype(jnp.bfloat16)

    smalls[3].wait()
    smalls[4].wait()
    slots = []
    mine_ids = jnp.full((live_rows, HD), steps, jnp.int32)
    for b in range(batch):
        seen = fill[b]
        slots_b = []
        for s in range(steps):
            mine = owner[s, b] == me
            slots_b.append(jnp.where(mine, seen, -1))
            seen = seen + jnp.where(mine, 1, 0)
            mine_ids = jnp.where(lane == s * batch + b, jnp.where(mine, s, steps), mine_ids)
        slots.append(slots_b)
    visible = mine_ids <= step_ids
    new_live = [visible & (lax.rem(lane, batch) == b) for b in range(batch)]

    peers = [partner(me, e, n_ctx) for e in range(n_ctx)]
    firsts = [None] + [
        pltpu.make_async_remote_copy(
            src_ref=send1.at[e], dst_ref=recv1.at[e], send_sem=ssem1.at[e], recv_sem=rsem1.at[e],
            device_id={"ctx": peers[e]}, device_id_type=MESH,
        )
        for e in range(1, n_ctx)
    ]
    all_b = range(batch)
    far_first = list(range(kv_local))[::-1]
    per_group = n_ctx // kv_local
    for turn in far_first:
        g = partner(lax.div(me, per_group), turn, kv_local)
        cols = pl.ds(pl.multiple_of(g * HD, HD), HD)
        nk_g = nk_f[:, cols].astype(jnp.bfloat16)
        nv_g = nv_f[:, cols].astype(jnp.bfloat16)
        at = [pl.ds(g * groups * tokens + b, live_rows, stride=batch) for b in all_b]
        query = [q_rows[at[b], :].astype(jnp.bfloat16) for b in all_b]
        if turn == far_first[0]:
            for copy in k_in:
                copy.wait()
        scores = [
            lax.dot_general(
                query[b], k_v[b, :, cols], (((1,), (1,)), ((), ())),
                preferred_element_type=jnp.float32,
            )
            for b in all_b
        ]
        new_scores = [
            lax.dot_general(
                query[b], nk_g, (((1,), (1,)), ((), ())), preferred_element_type=jnp.float32
            )
            for b in all_b
        ]
        masked = [
            jnp.where(slot_ids < fill[b], scores[b] * (1.0 / HD**0.5), -1e30) for b in all_b
        ]
        new_masked = [
            jnp.where(new_live[b], new_scores[b] * (1.0 / HD**0.5), -1e30) for b in all_b
        ]
        peak = [
            jnp.maximum(
                jnp.max(masked[b], axis=1, keepdims=True),
                jnp.max(new_masked[b], axis=1, keepdims=True),
            )
            for b in all_b
        ]
        weights = [jnp.exp(masked[b] - peak[b]) for b in all_b]
        new_weights = [jnp.exp(new_masked[b] - peak[b]) for b in all_b]
        total = [
            jnp.sum(weights[b], axis=1, keepdims=True)
            + jnp.sum(new_weights[b], axis=1, keepdims=True)
            for b in all_b
        ]
        if turn == far_first[0]:
            for copy in v_in:
                copy.wait()
        sums = [
            jnp.dot(
                weights[b].astype(jnp.bfloat16), v_v[b, :, cols],
                preferred_element_type=jnp.float32,
            )
            + jnp.dot(
                new_weights[b].astype(jnp.bfloat16), nv_g, preferred_element_type=jnp.float32
            )
            for b in all_b
        ]
        for b in all_b:
            part[at[b], :] = sums[b]
        for b in all_b:
            both = jnp.where(even, peak[b], total[b])
            high = both.astype(jnp.bfloat16).astype(jnp.float32)
            middle = (both - high).astype(jnp.bfloat16).astype(jnp.float32)
            low = both - high - middle
            stat[at[b], :] = jnp.where(lane < 2, high, jnp.where(lane < 4, middle, low))
        group = range((turn + 1) * per_group - 1, turn * per_group - 1, -1)
        for e in group:
            here = pl.ds(pl.multiple_of(peers[e] * block, 8), block)
            to = send1 if e else recv1
            to[e, 0:block, :] = part[here, :].astype(jnp.bfloat16)
            turned = lax.dot_general(
                pick, stat[here, :].astype(jnp.bfloat16), (((1,), (1,)), ((), ())),
                preferred_element_type=jnp.float32,
            )
            to[e, block : block + STAT_ROWS, 0:block] = turned.astype(jnp.bfloat16)
        if turn == far_first[0]:
            pl.semaphore_wait(barrier, n_ctx + n_head - 2)
        for e in group:
            if e:
                firsts[e].start()

    own_rows = [[s * batch + b for s in range(steps)] for b in all_b]
    for b in all_b:
        k_out[b] = new_rows(k_v[b], slots[b], nk_f, own_rows[b])

    for e in range(1, n_ctx):
        firsts[e].wait_recv()
    peaks, totals = [], []
    for d in range(n_ctx):
        got = recv1[d, block : block + STAT_ROWS, 0:block].astype(jnp.float32)
        peaks.append(got[0:1] + got[2:3] + got[4:5])
        totals.append(got[1:2] + got[3:4] + got[5:6])
    peaks = jnp.concatenate(peaks, axis=0)
    totals = jnp.concatenate(totals, axis=0)
    factor = jnp.exp(peaks - jnp.max(peaks, axis=0, keepdims=True))
    shares = factor / jnp.sum(factor * totals, axis=0, keepdims=True)
    shares = jnp.transpose(shares)
    attention = jnp.zeros((block, HD), jnp.float32)
    for d in range(n_ctx):
        attention += recv1[d, 0:block, :].astype(jnp.float32) * shares[:, d : d + 1]
    send2[...] = attention.astype(jnp.bfloat16)

    seconds = {}
    for d in range(n_ctx - 1, 0, -1):
        seconds[d] = pltpu.make_async_remote_copy(
            src_ref=send2, dst_ref=recv2.at[d], send_sem=ssem2.at[d], recv_sem=rsem2.at[d],
            device_id={"ctx": peers[d]}, device_id_type=MESH,
        )
        seconds[d].start()
    for b in all_b:
        v_out[b] = new_rows(v_v[b], slots[b], nv_f, own_rows[b])
    for copy in w_in:
        copy.wait()
    order = list(range(n_ctx))
    share = None
    for d in order:
        if d > 0:
            seconds[d].wait_recv()
            got = recv2[d].astype(jnp.float32)
        else:
            got = send2[...].astype(jnp.float32)
        features = jnp.concatenate(
            [got[i * tokens : (i + 1) * tokens] for i in range(per)], axis=1
        ).astype(jnp.bfloat16)
        source = peers[d]
        if d == order[-1]:
            break
        product = jnp.dot(features, w_v[source], preferred_element_type=jnp.float32)
        share = product if share is None else share + product
    for h in range(n_head):
        send3[h] = share[:, h * width : (h + 1) * width]
    third = []
    for e in range(n_head - 1, -1, -1):
        target = partner(hme, e, n_head)
        columns = pl.ds(pl.multiple_of(target * width, width), width)
        value = send3[target] + jnp.dot(
            features, w_v[source, :, columns], preferred_element_type=jnp.float32
        )
        if e == 0:
            result = value
            continue
        if e == 1:
            send3[target] = value
            origin, landing = send3.at[target], recv3
        else:
            stacked = [value[:, i * HD : (i + 1) * HD] for i in range(width // HD)]
            send4[e] = jnp.concatenate(stacked, axis=0).astype(jnp.bfloat16)
            origin, landing = send4.at[e], recv4.at[e]
        copy = pltpu.make_async_remote_copy(
            src_ref=origin, dst_ref=landing, send_sem=ssem3.at[e], recv_sem=rsem3.at[e],
            device_id={"head": target}, device_id_type=MESH,
        )
        copy.start()
        third.append(copy)
    for copy in third:
        copy.wait_recv()
    result += recv3[...]
    for e in range(2, n_head):
        got = recv4[e].astype(jnp.float32)
        result += jnp.concatenate(
            [got[i * tokens : (i + 1) * tokens] for i in range(width // HD)], axis=1
        )
    result = result.astype(mixed.dtype)
    for s in range(steps):
        mixed[s] = result[s * batch : (s + 1) * batch]

    for copy in firsts[1:]:
        copy.wait_send()
    for copy in seconds.values():
        copy.wait_send()
    for copy in third:
        copy.wait_send()


def write_kernel(k_in, v_in, m_in, k_out, v_out, m_out, sems):
    batch = k_in.shape[0]
    copies = [pltpu.make_async_copy(m_in, m_out, sems.at[2 * batch])]
    for b in range(batch):
        copies.append(pltpu.make_async_copy(k_in.at[b], k_out.at[b], sems.at[b]))
        copies.append(pltpu.make_async_copy(v_in.at[b], v_out.at[b], sems.at[batch + b]))
    for copy in copies:
        copy.start()
    for copy in copies:
        copy.wait()


def on_device_fused(
    n_ctx, n_head, queries, k_cache, v_cache, new_keys, new_values, fill, owner, out_weight
):
    steps, batch, features = queries.shape
    rows, kv_width = k_cache.shape[1:]
    kv_local = kv_width // HD
    heads = features // HD
    tokens = steps * batch
    columns = out_weight.shape[1]
    per = heads // n_ctx
    block = per * tokens
    if heads % n_ctx or block % 16 or block > HD or n_ctx % kv_local or batch != 8 or n_ctx & (n_ctx - 1) or n_head & (n_head - 1) or n_head < 2 or kv_local & (kv_local - 1) or tokens > HD or columns % (n_head * HD):
        return on_device(
            queries, k_cache, v_cache, new_keys, new_values, fill, owner, out_weight
        )
    kernel = functools.partial(
        fused_kernel, n_ctx, n_head, steps, batch, heads // kv_local, kv_local
    )
    whole = pl.BlockSpec(memory_space=pl.ANY)
    dma = pltpu.SemaphoreType.DMA
    shapes = (
        jax.ShapeDtypeStruct(k_cache.shape, k_cache.dtype),
        jax.ShapeDtypeStruct(v_cache.shape, v_cache.dtype),
        jax.ShapeDtypeStruct((steps, batch, columns // n_head), jnp.bfloat16),
    )
    results = pl.pallas_call(
        kernel,
        out_shape=shapes,
        in_specs=[whole] * 8,
        out_specs=(pl.BlockSpec(memory_space=pltpu.VMEM),) * 3,
        scratch_shapes=[
            pltpu.SMEM((batch,), jnp.int32),
            pltpu.SMEM((steps, batch), jnp.int32),
            pltpu.VMEM(queries.shape, jnp.bfloat16),
            pltpu.VMEM(new_keys.shape, jnp.bfloat16),
            pltpu.VMEM(new_values.shape, jnp.bfloat16),
            pltpu.VMEM(k_cache.shape, jnp.bfloat16),
            pltpu.VMEM(v_cache.shape, jnp.bfloat16),
            pltpu.VMEM((n_ctx, per * HD, columns), jnp.bfloat16),
            pltpu.VMEM((heads * tokens, HD), jnp.float32),
            pltpu.VMEM((heads * tokens, HD), jnp.float32),
            pltpu.VMEM((heads * tokens, HD), jnp.float32),
            pltpu.VMEM((HD, kv_width), jnp.float32),
            pltpu.VMEM((HD, kv_width), jnp.float32),
            pltpu.VMEM((n_ctx, block + STAT_ROWS, HD), jnp.bfloat16),
            pltpu.VMEM((n_ctx, block + STAT_ROWS, HD), jnp.bfloat16),
            pltpu.VMEM((block, HD), jnp.bfloat16),
            pltpu.VMEM((n_ctx, block, HD), jnp.bfloat16),
            pltpu.VMEM((n_head, tokens, columns // n_head), jnp.float32),
            pltpu.VMEM((tokens, columns // n_head), jnp.float32),
            pltpu.VMEM((n_head, tokens * columns // n_head // HD, HD), jnp.bfloat16),
            pltpu.VMEM((n_head, tokens * columns // n_head // HD, HD), jnp.bfloat16),
            dma((5,)),
            dma((batch,)),
            dma((batch,)),
            dma((n_ctx,)),
            dma((n_ctx,)),
            dma((n_ctx,)),
            dma((n_ctx,)),
            dma((n_ctx,)),
            dma((n_head,)),
            dma((n_head,)),
        ],
        compiler_params=pltpu.CompilerParams(
            collective_id=0, has_side_effects=True, vmem_limit_bytes=VMEM_BYTES
        ),
        cost_estimate=pl.CostEstimate(
            flops=2 * tokens * features * (columns + 2 * rows),
            bytes_accessed=2 * (2 * k_cache.size + 2 * v_cache.size + out_weight.size),
            transcendentals=tokens * heads * rows,
        ),
    )(*[
        pltpu.with_memory_space_constraint(x, pltpu.HBM)
        for x in (
            fill.reshape(batch), owner, queries, k_cache, v_cache, new_keys, new_values, out_weight
        )
    ])
    return pl.pallas_call(
        write_kernel,
        out_shape=shapes,
        in_specs=[whole] * 3,
        out_specs=(whole,) * 3,
        scratch_shapes=[dma((2 * batch + 1,))],
        compiler_params=pltpu.CompilerParams(vmem_limit_bytes=1024 * 1024),
    )(*[pltpu.with_memory_space_constraint(x, pltpu.VMEM) for x in results])


def solution(mesh):
    in_specs = (
        P(None, None, "head"),
        P(None, "ctx", "head"),
        P(None, "ctx", "head"),
        P(None, None, "head"),
        P(None, None, "head"),
        P(None, "ctx"),
        P(),
        P("head", "ctx"),
    )
    out_specs = (P(None, "ctx", "head"), P(None, "ctx", "head"), P(None, None, ("ctx", "head")))
    return jax.shard_map(
        functools.partial(on_device_fused, mesh.shape["ctx"], mesh.shape["head"]), mesh=mesh, in_specs=in_specs, out_specs=out_specs, check_vma=False
    )
```
